32 devices in a mesh: grp: 4 (over y, core), dev: 8 (over z, x).
Axes of the slice: x: 2, y: 2, z: 4, core: 2. Of those that a mesh axis runs over, the one named last changes fastest.
Arguments:
- charges: bfloat16 [1024, 16, 128], P(('grp', 'dev')), may hold values from -6 to 6
- leaf_basis: bfloat16 [1024, 128, 64], P(('grp', 'dev')), may hold values from -0.5 to 0.5
- near_blocks: bfloat16 [5120, 128, 128], P(('grp', 'dev')), may hold values from -0.375 to 0.375
- near_target: int32 [5120], P(('grp', 'dev')), may hold values from 0 to 1023, as said below
- near_source: int32 [5120], P(('grp', 'dev')), may hold values from 0 to 1023, as said below
- near_count: int32 [32], P(('grp', 'dev')), may hold values from 40 to 160, as said below
- leaf_far: int32 [1024, 16], P(('grp', 'dev')), may hold values from 0 to 1023, as said below
- leaf_far_couple: int32 [1024, 16], P(('grp', 'dev')), may hold values from 0 to 315
- leaf_trans: int32 [1024], P(('grp', 'dev')), may hold values from 0 to 7
- dev_trans: int32 [32], P(('grp', 'dev')), may hold values from 0 to 7
- dev_list: int32 [32, 4], P(('grp', 'dev')), may hold values from 0 to 31, as said below
- dev_couple: int32 [32, 4], P(('grp', 'dev')), may hold values from 0 to 315
- grp_couple: int32 [4, 4], replicated, may hold values from 0 to 315
- trans_leaf: float32 [8, 64, 64], replicated, may hold values from -0.375 to 0.375
- trans_dev: float32 [8, 64, 64], replicated, may hold values from -0.25 to 0.25
- couple_table: float32 [316, 64, 64], replicated, may hold values from -0.375 to 0.375
Outputs:
- potentials: float32 [1024, 16, 128], P(('grp', 'dev'))
The draws below stay inside these ranges and needn't reach their ends.
Inputs may be any that keep to these rules, and one draw needn't show every extreme that they name: `near_count`: live slots of a device are at least a quarter of its 160; some device has all slots live and some device exactly 40. `near_target`: slot s names a leaf of device s // 160. `near_source`: slot s names a leaf within 16 leaves of device s // 160's range of leaves; on every device both ends of that window are named where they exist. `leaf_far`: leaf b names leaves within 16 leaves of the range of its device; on every device both ends of that window are named where they exist. `dev_list`: box d names boxes of its own subtree, never itself nor the two next to it in cyclic order within the subtree.
All inputs are finite; a program needn't handle non-finite values.
Results may differ from the reference program's by a relative error of at most 0.0024.
Values may be sent and summed in bfloat16 or wider, within the bound.
No kernel may reach another device: no remote copies, remote signals or barrier semaphores. Data moves between devices by JAX's collectives and lax.ppermute only.
A program may use at most 128 MiB of HBM per device.

```python
import jax
import jax.numpy as jnp
from jax import lax

R = 16
P_SIZE = 128
K = 64
NTRANS = 8
NCOUPLE = 316
NFAR = 16
NL1 = 4
LEAF_DEV = 32
NB_DEV = 160
HALO = 16
GROUPS = 4
GDEV = 8
BOXES = 32
NLEAF = 1024


def window_sources(key, rows, per_row, per_device):
    device_of = (jnp.arange(rows) // per_device).astype(jnp.int32)
    lowest = device_of * LEAF_DEV - HALO
    highest = device_of * LEAF_DEV + LEAF_DEV + HALO - 1
    offsets = jax.random.randint(key, (rows, per_row), 0, LEAF_DEV + 2 * HALO)
    values = lowest[:, None] + offsets
    row_local = (jnp.arange(rows) % per_device)[:, None]
    column = jnp.arange(per_row)[None, :]
    return (values, lowest, highest, row_local, column)


def draw_near_count(key, part):
    first_key, second_key, third_key = jax.random.split(jax.random.fold_in(key, 11), 3)
    counts = NB_DEV // 4 + jax.random.randint(first_key, (BOXES,), 0, NB_DEV - NB_DEV // 4 + 1)
    busiest = jax.random.randint(second_key, (), 0, BOXES)
    lightest = (busiest + 1 + jax.random.randint(third_key, (), 0, BOXES - 1)) % BOXES
    counts = counts.at[busiest].set(NB_DEV)
    counts = counts.at[lightest].set(NB_DEV // 4)
    return counts.astype(jnp.int32)


def draw_near_target(key, part):
    slots = BOXES * NB_DEV
    device_of = (jnp.arange(slots) // NB_DEV).astype(jnp.int32)
    offsets = jax.random.randint(jax.random.fold_in(key, 12), (slots,), 0, LEAF_DEV)
    local_slot = jnp.arange(slots) % NB_DEV
    offsets = jnp.where(local_slot == 0, 0, jnp.where(local_slot == 1, LEAF_DEV - 1, offsets))
    return (device_of * LEAF_DEV + offsets).astype(jnp.int32)


def draw_near_source(key, part):
    slots = BOXES * NB_DEV
    values, lowest, highest, row_local, column = window_sources(jax.random.fold_in(key, 13), slots, 1, NB_DEV)
    values = values[:, 0]
    values = jnp.where(row_local[:, 0] == 0, lowest, jnp.where(row_local[:, 0] == 1, highest, values))
    return jnp.clip(values, 0, NLEAF - 1).astype(jnp.int32)


def draw_leaf_far(key, part):
    values, lowest, highest, row_local, column = window_sources(jax.random.fold_in(key, 14), NLEAF, NFAR, LEAF_DEV)
    values = jnp.where((row_local == 0) & (column == 0), lowest[:, None], values)
    values = jnp.where((row_local == LEAF_DEV - 1) & (column == NFAR - 1), highest[:, None], values)
    return jnp.clip(values, 0, NLEAF - 1).astype(jnp.int32)


def draw_dev_list(key, part):
    box_ids = jnp.arange(BOXES).astype(jnp.int32)
    subtree = box_ids // GDEV
    member = box_ids % GDEV
    offsets = jax.random.randint(jax.random.fold_in(key, 15), (BOXES, NL1), 0, GDEV - 3)
    chosen = (member[:, None] + 2 + offsets) % GDEV
    return (subtree[:, None] * GDEV + chosen).astype(jnp.int32)


def touch_ends(entries, stream_key, smallest, top_value):
    dims = entries.shape
    index_at = [jax.random.randint(jax.random.fold_in(stream_key, axis), (), 0, dims[axis]) for axis in range(len(dims))]
    entries = entries.at[tuple(index_at)].set(smallest)
    longest = dims.index(max(dims))
    index_at[longest] = (index_at[longest] + 1) % dims[longest]
    return entries.at[tuple(index_at)].set(top_value)


def block_levels(rng, dims, shards, smallest, top_value):
    loudness, own = 1.0, jax.random.fold_in(rng, 6)
    for position, shards_of in shards:
        draws = jnp.exp(jax.random.uniform(jax.random.fold_in(own, position), (shards_of,), jnp.float32, smallest / len(shards), top_value / len(shards)))
        loudness = loudness * jnp.repeat(draws, dims[position] // shards_of).reshape([-1 if axis == position else 1 for axis in range(len(dims))])
    return loudness


def bell_draw(stream_key, shape, width, bound, pieces=(), kind=jnp.bfloat16):
    gain = block_levels(stream_key, shape, pieces, -0.22, 0.18) if pieces else 1.0
    entries = jax.random.normal(stream_key, shape, jnp.float32) * width * gain
    return jnp.minimum(jnp.maximum(entries, -bound), bound).astype(kind)


def setup_inputs(seed: int = 0) -> dict:
    streams_of = jax.random.split(jax.random.key(seed), 17)
    return {
        "charges": bell_draw(streams_of[0], (NLEAF, R, P_SIZE), 1.0, 6.0, ((0, 32),)),
        "leaf_basis": bell_draw(streams_of[1], (NLEAF, P_SIZE, K), P_SIZE ** -0.5, 0.5, ((0, 32),)),
        "near_blocks": bell_draw(streams_of[2], (BOXES * NB_DEV, P_SIZE, P_SIZE), (2 * P_SIZE) ** -0.5, 0.375, ((0, 32),)),
        "near_target": draw_near_target(jax.random.fold_in(streams_of[16], 71), 0),
        "near_source": draw_near_source(jax.random.fold_in(streams_of[16], 71), 0),
        "near_count": draw_near_count(jax.random.fold_in(streams_of[16], 71), 0),
        "leaf_far": draw_leaf_far(jax.random.fold_in(streams_of[16], 71), 0),
        "leaf_far_couple": touch_ends(jax.random.randint(streams_of[7], (NLEAF, NFAR), 0, NCOUPLE), jax.random.fold_in(streams_of[7], 1), 0, NCOUPLE - 1).astype(jnp.int32),
        "leaf_trans": touch_ends(jax.random.randint(streams_of[8], (NLEAF,), 0, NTRANS), jax.random.fold_in(streams_of[8], 1), 0, NTRANS - 1).astype(jnp.int32),
        "dev_trans": touch_ends(jax.random.randint(streams_of[9], (BOXES,), 0, NTRANS), jax.random.fold_in(streams_of[9], 1), 0, NTRANS - 1).astype(jnp.int32),
        "dev_list": draw_dev_list(jax.random.fold_in(streams_of[16], 71), 0),
        "dev_couple": touch_ends(jax.random.randint(streams_of[11], (BOXES, NL1), 0, NCOUPLE), jax.random.fold_in(streams_of[11], 1), 0, NCOUPLE - 1).astype(jnp.int32),
        "grp_couple": touch_ends(jax.random.randint(streams_of[12], (GROUPS, GROUPS), 0, NCOUPLE), jax.random.fold_in(streams_of[12], 1), 0, NCOUPLE - 1).astype(jnp.int32),
        "trans_leaf": bell_draw(streams_of[13], (NTRANS, K, K), (4 * K) ** -0.5, 0.375, (), jnp.float32),
        "trans_dev": bell_draw(streams_of[14], (NTRANS, K, K), (8 * K) ** -0.5, 0.25, (), jnp.float32),
        "couple_table": bell_draw(streams_of[15], (NCOUPLE, K, K), (4 * K) ** -0.5, 0.375, (), jnp.float32),
    }


HIGHEST = lax.Precision.HIGHEST


def reference(charges, leaf_basis, near_blocks, near_target, near_source, near_count, leaf_far, leaf_far_couple, leaf_trans, dev_trans, dev_list, dev_couple, grp_couple, trans_leaf, trans_dev, couple_table):
    f32 = jnp.float32
    basis_wide = leaf_basis.astype(f32)
    leaf_moment = jnp.einsum('lrp,lpk->lrk', charges.astype(f32), basis_wide, precision=HIGHEST)
    child_maps = trans_leaf[leaf_trans].reshape(BOXES, LEAF_DEV, K, K)
    box_moment = jnp.einsum('blrk,blkj->brj', leaf_moment.reshape(BOXES, LEAF_DEV, R, K), child_maps, precision=HIGHEST)
    up_maps = trans_dev[dev_trans]
    group_moment = jnp.einsum('gdrk,gdkj->grj', box_moment.reshape(GROUPS, GDEV, R, K), up_maps.reshape(GROUPS, GDEV, K, K), precision=HIGHEST)
    away = 1.0 - jnp.eye(GROUPS, dtype=f32)
    group_local = jnp.einsum('gh,hrk,ghkj->grj', away, group_moment, couple_table[grp_couple], precision=HIGHEST)
    owner_group = jnp.arange(BOXES) // GDEV
    box_local = jnp.einsum('brj,bkj->brk', group_local[owner_group], up_maps, precision=HIGHEST)
    box_local = box_local + jnp.einsum('bnrk,bnkj->brj', box_moment[dev_list], couple_table[dev_couple], precision=HIGHEST)
    leaf_local = jnp.einsum('brj,blkj->blrk', box_local, child_maps, precision=HIGHEST).reshape(NLEAF, R, K)

    def far_box(inputs):
        sources, kinds = inputs
        return jnp.einsum('lfrk,lfkj->lrj', leaf_moment[sources], couple_table[kinds], precision=HIGHEST)

    far_terms = lax.map(far_box, (leaf_far.reshape(BOXES, LEAF_DEV, NFAR), leaf_far_couple.reshape(BOXES, LEAF_DEV, NFAR)))
    leaf_local = (leaf_local + far_terms.reshape(NLEAF, R, K)).astype(jnp.bfloat16)
    far_part = jnp.einsum('lrk,lpk->lrp', leaf_local.astype(f32), basis_wide, precision=HIGHEST)

    def near_box(inputs):
        blocks, targets, sources, count, box_index = inputs
        picked = charges[sources].astype(f32)
        product = jnp.einsum('sij,srj->sri', blocks.astype(f32), picked, precision=HIGHEST)
        live = jnp.arange(NB_DEV) < count
        local_target = targets - box_index * LEAF_DEV
        onehot = ((local_target[None, :] == jnp.arange(LEAF_DEV)[:, None]) & live[None, :]).astype(f32)
        return jnp.einsum('ts,sri->tri', onehot, product, precision=HIGHEST)

    near_terms = lax.map(near_box, (near_blocks.reshape(BOXES, NB_DEV, P_SIZE, P_SIZE), near_target.reshape(BOXES, NB_DEV), near_source.reshape(BOXES, NB_DEV), near_count, jnp.arange(BOXES).astype(jnp.int32)))
    return near_terms.reshape(NLEAF, R, P_SIZE) + far_part
```

```python
import functools

import jax
import jax.numpy as jnp
from jax import lax
from jax.experimental import pallas as pl
from jax.experimental.pallas import tpu as pltpu
from jax.sharding import PartitionSpec as P

HIGHEST = lax.Precision.HIGHEST
F32 = jnp.float32
BF16 = jnp.bfloat16
NT = (((1,), (1,)), ((), ()))
AXES = ("grp", "dev")
VMEM = pl.BlockSpec(memory_space=pltpu.VMEM)
SMEM = pl.BlockSpec(memory_space=pltpu.SMEM)
ANY = pl.BlockSpec(memory_space=pl.ANY)
MIB = 2**20


def halves(x):
    half = x.shape[1] // 2
    return jnp.concatenate([x[:, :half], x[:, half:]], axis=0)


def fold(product):
    r, j = product.shape[0] // 2, product.shape[1] // 2
    return product[:r, :j] + product[r:, j:]


def moment_kernel(
    leaf_trans, dev_trans, charges, basis_t, trans_leaf, trans_dev,
    moments, send_first, send_second, sums, classes,
):
    leaves, r, _ = charges.shape
    k = basis_t.shape[1]
    margin = leaves // 2
    kinds = trans_leaf.shape[0]
    even = lax.rem(lax.axis_index("dev"), 2) == 0
    left = lax.broadcasted_iota(jnp.int32, (r, 2 * k), 1) < k
    classes[...] = jnp.zeros_like(classes)
    for leaf in range(leaves):
        basis = basis_t[leaf]
        twice = lax.dot_general(
            charges[leaf], jnp.concatenate([basis, basis], axis=0), NT,
            preferred_element_type=F32,
        )
        kind = leaf_trans[leaf]
        classes[kind] = classes[kind] + twice
        high = twice.astype(BF16).astype(F32)
        moments[leaf] = jnp.where(left, high, twice - high).astype(BF16)
    own = functools.partial(jnp.dot, precision=HIGHEST, preferred_element_type=F32)
    box = jnp.zeros((r, k), F32)
    for pair in range(kinds // 2):
        lhs = jnp.where(left, classes[2 * pair], classes[2 * pair + 1])
        rhs = jnp.concatenate([trans_leaf[2 * pair], trans_leaf[2 * pair + 1]], axis=0)
        box = box + own(lhs, rhs)
    up = own(box, trans_dev[dev_trans[0]])
    both = jnp.concatenate([box, up], axis=0)
    wide = jnp.concatenate([both, jnp.zeros_like(both)], axis=1)
    sums[...] = wide
    high = wide.astype(BF16)
    send_first[margin] = high
    send_first[margin + 1] = (wide - high.astype(F32)).astype(BF16)

    def fill(first_from, second_from):
        for leaf in range(margin):
            send_first[leaf, :r] = charges[first_from + leaf]
            send_first[leaf, r:] = moments[first_from + leaf]
            send_second[leaf, :r] = charges[second_from + leaf]
            send_second[leaf, r:] = moments[second_from + leaf]

    @pl.when(even)
    def _():
        fill(margin, 0)

    @pl.when(jnp.logical_not(even))
    def _():
        fill(0, margin)


def table_kernel(steps, table, out, buffer, sems):
    half, kinds = buffer.shape[1], buffer.shape[3]
    size = half // steps
    copies = [
        pltpu.make_async_copy(
            table.at[:, pl.ds(i * size, size)], buffer.at[:, pl.ds(i * size, size)], sems.at[i]
        )
        for i in range(steps)
    ]
    for copy in copies:
        copy.start()
    for i, copy in enumerate(copies):
        copy.wait()

        def step(row, carry):
            stacked = jnp.concatenate([buffer[0, row], buffer[1, row]], axis=0)
            for start in range(0, kinds, 128):
                width = min(128, kinds - start)
                out[pl.ds(start * half + row, width, stride=half), :] = stacked[
                    :, start : start + width
                ].T
            return carry

        lax.fori_loop(i * size, (i + 1) * size, step, 0, unroll=4)


def near_kernel(
    chunk, unroll, targets, sources, count, charges, first, second, blocks,
    out, window, buffer, total, sems,
):
    slots = blocks.shape[0]
    leaves, r, _ = charges.shape
    margin = leaves // 2
    live = count[0]
    leaf_start = (lax.axis_index("grp") * lax.axis_size("dev") + lax.axis_index("dev")) * leaves
    even = lax.rem(lax.axis_index("dev"), 2) == 0
    copies = [
        pltpu.make_async_copy(
            blocks.at[pl.ds(i * chunk, chunk)], buffer.at[pl.ds(i * chunk, chunk)], sems.at[i]
        )
        for i in range(slots // chunk)
    ]
    for i, copy in enumerate(copies):

        @pl.when(i * chunk < live)
        def _():
            copy.start()

    low_at = jnp.where(even, margin + leaves, 0)
    high_at = jnp.where(even, 0, margin + leaves)
    window[pl.ds(margin, leaves)] = charges[...]
    window[pl.ds(low_at, margin)] = first[:margin, :r]
    window[pl.ds(high_at, margin)] = second[:, :r]
    total[...] = jnp.zeros_like(total)
    for i, copy in enumerate(copies):

        @pl.when(i * chunk < live)
        def _():
            copy.wait()

            def step(group, carry):
                base = i * chunk + group * unroll
                products = [
                    lax.dot_general(
                        window[sources[base + u] - leaf_start + margin], buffer[base + u], NT,
                        preferred_element_type=F32,
                    )
                    for u in range(unroll)
                ]
                for u in range(unroll):
                    slot = base + u
                    row = jnp.where(slot < live, targets[slot] - leaf_start, leaves)
                    total[row] = total[row] + products[u]
                return carry

            here = jnp.minimum(live - i * chunk, chunk)
            lax.fori_loop(0, (here + unroll - 1) // unroll, step, 0)

    out[...] = total[:leaves]


def far_kernel(
    boxes_count, far, far_couple, dev_list, dev_couple, grp_couple, moments, first, second,
    table, *rest,
):
    boxes = rest[:boxes_count]
    out, listed_out, group_tables, window, spread, gathered = rest[boxes_count:]
    leaves, r, width = moments.shape
    margin = leaves // 2
    nfar = far.shape[0]
    half = width // 4
    group = lax.axis_index("grp")
    per_group = lax.axis_size("dev")
    member = lax.axis_index("dev")
    leaf_start = (group * per_group + member) * leaves
    even = lax.rem(member, 2) == 0
    low_at = jnp.where(even, margin + leaves, 0)
    high_at = jnp.where(even, 0, margin + leaves)
    window[pl.ds(margin, leaves)] = moments[...]
    window[pl.ds(low_at, margin)] = first[:margin, r:]
    window[pl.ds(high_at, margin)] = second[:, r:]
    row = lax.broadcasted_iota(jnp.int32, (width, 4 * width), 0)
    column = lax.broadcasted_iota(jnp.int32, (width, 4 * width), 1)
    copier = (row == (column // width) * half + lax.rem(column, half)).astype(BF16)
    piece = 8
    for start in range(0, 2 * leaves, piece):
        rows = window[start : start + piece].reshape(piece * r, width)
        copied = jnp.dot(rows, copier, preferred_element_type=F32).astype(BF16)
        for section in range(4):
            spread[start : start + piece, section * r : (section + 1) * r] = copied[
                :, section * width : (section + 1) * width
            ].reshape(piece, r, width)
    lane = lax.broadcasted_iota(jnp.int32, (4 * r, width), 1) // half

    def couple(kind):
        return table[pl.ds(pl.multiple_of(kind * half, half), half), :]

    def one(leaf):
        lhs, rhs = [], []
        for quad in range(nfar // 4):
            picked = None
            tables = []
            for q in range(4):
                f = quad * 4 + q
                source = spread[far[f, leaf] - leaf_start + margin]
                picked = source if q == 0 else jnp.where(lane >= q, source, picked)
                tables.append(couple(far_couple[f, leaf]))
            stacked = jnp.concatenate(tables, axis=0)
            high = stacked.astype(BF16)
            low = (stacked - high.astype(F32)).astype(BF16)
            lhs.append(picked)
            rhs.append(jnp.concatenate([high, low], axis=1))
        product = jnp.dot(
            jnp.concatenate(lhs, axis=1), jnp.concatenate(rhs, axis=0),
            preferred_element_type=F32,
        )
        product = product[: 2 * r] + product[2 * r :]
        return fold(product[:, :width] + product[:, width:])

    def step(index, carry):
        results = [one(index * 2 + u) for u in range(2)]
        for u in range(2):
            out[index * 2 + u] = results[u]
        return carry

    lax.fori_loop(0, leaves // 2, step, 0)
    for pair in range(boxes_count):
        for e in range(2):
            gathered[2 * pair + e] = boxes[pair][e, :r]
    lhs, rhs = [], []
    for n in range(dev_list.shape[1]):
        place = jnp.bitwise_xor(dev_list[0, n] - group * per_group, member)
        lhs.append(halves(gathered[place][:, : 2 * half]))
        rhs.append(couple(dev_couple[0, n]))
    listed_out[...] = fold(
        jnp.dot(
            jnp.concatenate(lhs, axis=1), jnp.concatenate(rhs, axis=0),
            precision=HIGHEST, preferred_element_type=F32,
        )
    )
    for other in range(1, grp_couple.shape[0]):
        group_tables[other - 1] = couple(grp_couple[group, jnp.bitwise_xor(group, other)])


def final_kernel(
    others, leaf_trans, dev_trans, near, far, listed, group_tables, basis_t, trans_leaf,
    trans_dev, *rest,
):
    groups = rest[:others]
    out, locals_ = rest[others:]
    own = functools.partial(lax.dot_general, precision=HIGHEST, preferred_element_type=F32)
    group_local = None
    for other in range(others):
        term = fold(
            jnp.dot(
                halves(groups[other][...]), group_tables[other],
                precision=HIGHEST, preferred_element_type=F32,
            )
        )
        group_local = term if other == 0 else group_local + term
    box_local = own(group_local, trans_dev[dev_trans[0]], NT) + listed[...]
    for kind in range(trans_leaf.shape[0]):
        locals_[kind] = own(box_local, trans_leaf[kind], NT)
    for leaf in range(near.shape[0]):
        leaf_local = (locals_[leaf_trans[leaf]] + far[leaf]).astype(BF16)
        out[leaf] = near[leaf] + jnp.dot(
            leaf_local, basis_t[leaf], preferred_element_type=F32
        )


def swap(x, axis, distance):
    return lax.ppermute(x, axis, [(i, i ^ distance) for i in range(lax.axis_size(axis))])


def params(mib):
    return pltpu.CompilerParams(vmem_limit_bytes=mib * MIB)


def local(
    charges,
    leaf_basis,
    near_blocks,
    near_target,
    near_source,
    near_count,
    leaf_far,
    leaf_far_couple,
    leaf_trans,
    dev_trans,
    dev_list,
    dev_couple,
    grp_couple,
    trans_leaf,
    trans_dev,
    couple_table,
):
    leaves, r, panels = charges.shape
    k = leaf_basis.shape[2]
    margin = leaves // 2
    slots = near_blocks.shape[0]
    kinds = couple_table.shape[0]
    half = k // 2
    per_group = lax.axis_size("dev")
    devices = per_group * lax.axis_size("grp")
    basis_t = jnp.swapaxes(leaf_basis, 1, 2)
    shape = jax.ShapeDtypeStruct

    moments, send_first, send_second, sums = pl.pallas_call(
        moment_kernel,
        out_shape=(
            shape((leaves, r, 2 * k), BF16),
            shape((margin + 2, 2 * r, panels), BF16),
            shape((margin, 2 * r, panels), BF16),
            shape((2 * r, 2 * k), F32),
        ),
        in_specs=[SMEM, SMEM, VMEM, VMEM, VMEM, VMEM],
        out_specs=(VMEM, VMEM, VMEM, VMEM),
        scratch_shapes=[pltpu.VMEM((trans_leaf.shape[0], r, 2 * k), F32)],
        compiler_params=params(16),
        name="moments",
    )(leaf_trans, dev_trans, charges, basis_t, trans_leaf, trans_dev)

    first = swap(send_first, "dev", 1)
    second = lax.ppermute(
        send_second,
        AXES,
        [(i, i + 1) for i in range(1, devices - 1, 2)]
        + [(i + 1, i) for i in range(1, devices - 1, 2)],
    )

    steps = 4
    table = pl.pallas_call(
        functools.partial(table_kernel, steps),
        out_shape=shape((kinds * half, 2 * k), F32),
        in_specs=[ANY],
        out_specs=VMEM,
        scratch_shapes=[
            pltpu.VMEM((2, half, k, kinds), F32),
            pltpu.SemaphoreType.DMA((steps,)),
        ],
        compiler_params=params(20),
        cost_estimate=pl.CostEstimate(flops=0, bytes_accessed=12 * MIB, transcendentals=0),
        name="table",
    )(jnp.transpose(couple_table, (1, 2, 0)).reshape(2, half, k, kinds))

    peer = first[margin].astype(F32) + first[margin + 1].astype(F32)
    pair = jnp.stack([sums, peer])
    pairs = [pair] + [swap(pair, "dev", distance) for distance in range(2, per_group, 2)]

    chunk = slots // 8
    near = pl.pallas_call(
        functools.partial(near_kernel, chunk, 4),
        out_shape=shape((leaves, r, panels), F32),
        in_specs=[SMEM, SMEM, SMEM, VMEM, VMEM, VMEM, ANY],
        out_specs=VMEM,
        scratch_shapes=[
            pltpu.VMEM((2 * leaves, r, panels), BF16),
            pltpu.VMEM(near_blocks.shape, BF16),
            pltpu.VMEM((leaves + 1, r, panels), F32),
            pltpu.SemaphoreType.DMA((slots // chunk,)),
        ],
        compiler_params=params(16),
        cost_estimate=pl.CostEstimate(flops=0, bytes_accessed=12 * MIB, transcendentals=0),
        name="near",
    )(near_target, near_source, near_count, charges, first, second, near_blocks)

    group_moment = sum(jnp.sum(part[:, r:, :k], axis=0) for part in pairs)
    groups = [
        swap(group_moment, "grp", distance) for distance in range(1, lax.axis_size("grp"))
    ]

    far, listed, group_tables = pl.pallas_call(
        functools.partial(far_kernel, len(pairs)),
        out_shape=(
            shape((leaves, r, k), F32),
            shape((r, k), F32),
            shape((len(groups), half, 2 * k), F32),
        ),
        in_specs=[SMEM] * 5 + [VMEM] * (4 + len(pairs)),
        out_specs=(VMEM, VMEM, VMEM),
        scratch_shapes=[
            pltpu.VMEM((2 * leaves, r, 2 * k), BF16),
            pltpu.VMEM((2 * leaves, 4 * r, 2 * k), BF16),
            pltpu.VMEM((2 * len(pairs), r, 2 * k), F32),
        ],
        compiler_params=params(16),
        cost_estimate=pl.CostEstimate(flops=0, bytes_accessed=12 * MIB, transcendentals=0),
        name="far",
    )(
        leaf_far.T, leaf_far_couple.T, dev_list, dev_couple, grp_couple,
        moments, first, second, table, *pairs,
    )

    return pl.pallas_call(
        functools.partial(final_kernel, len(groups)),
        out_shape=shape((leaves, r, panels), F32),
        in_specs=[SMEM, SMEM] + [VMEM] * (7 + len(groups)),
        out_specs=VMEM,
        scratch_shapes=[pltpu.VMEM((trans_leaf.shape[0], r, k), F32)],
        compiler_params=params(16),
        name="final",
    )(
        leaf_trans, dev_trans, near, far, listed, group_tables, basis_t, trans_leaf,
        trans_dev, *groups,
    )


def solution(mesh):
    leaf = P(AXES)
    return jax.shard_map(
        local,
        mesh=mesh,
        in_specs=(leaf,) * 12 + (P(),) * 4,
        out_specs=leaf,
        check_vma=False,
    )
```

```python
import functools

import jax
import jax.numpy as jnp
from jax import lax
from jax.experimental import pallas as pl
from jax.experimental.pallas import tpu as pltpu
from jax.sharding import PartitionSpec as P

HIGHEST = lax.Precision.HIGHEST
F32 = jnp.float32
BF16 = jnp.bfloat16
NT = (((1,), (1,)), ((), ()))
AXES = ("grp", "dev")
VMEM = pl.BlockSpec(memory_space=pltpu.VMEM)
SMEM = pl.BlockSpec(memory_space=pltpu.SMEM)
HBM = pl.BlockSpec(memory_space=pltpu.HBM)
MIB = 2**20


def halves(x):
    half = x.shape[1] // 2
    return jnp.concatenate([x[:, :half], x[:, half:]], axis=0)


def fold(product):
    r, j = product.shape[0] // 2, product.shape[1] // 2
    return product[:r, :j] + product[r:, j:]


def moment_kernel(
    leaf_trans_hbm, dev_trans_hbm, charges_hbm, basis_hbm, trans_leaf_hbm, trans_dev_hbm, table_hbm,
    moments, send_first, send_second, sums, charges, basis_t, trans_leaf, trans_dev, table,
    leaf_trans, dev_trans, classes, sems,
):
    moves = [
        (charges_hbm, charges), (basis_hbm, basis_t), (leaf_trans_hbm, leaf_trans),
        (trans_leaf_hbm, trans_leaf), (dev_trans_hbm, dev_trans), (trans_dev_hbm, trans_dev),
        (table_hbm, table),
    ]
    copies = [
        pltpu.make_async_copy(source, target, sems.at[i])
        for i, (source, target) in enumerate(moves)
    ]
    for copy in copies:
        copy.start()
    leaves, r, _ = charges.shape
    k = basis_t.shape[1]
    margin = leaves // 2
    kinds = trans_leaf.shape[0]
    even = lax.rem(lax.axis_index("dev"), 2) == 0
    left = lax.broadcasted_iota(jnp.int32, (r, 2 * k), 1) < k
    classes[...] = jnp.zeros_like(classes)
    for copy in copies[:3]:
        copy.wait()
    for leaf in range(leaves):
        basis = basis_t[leaf]
        twice = lax.dot_general(
            charges[leaf], jnp.concatenate([basis, basis], axis=0), NT,
            preferred_element_type=F32,
        )
        kind = leaf_trans[leaf]
        classes[kind] = classes[kind] + twice
        high = twice.astype(BF16).astype(F32)
        moments[leaf] = jnp.where(left, high, twice - high).astype(BF16)
    for copy in copies[3:6]:
        copy.wait()
    own = functools.partial(jnp.dot, precision=HIGHEST, preferred_element_type=F32)
    box = jnp.zeros((r, k), F32)
    for pair in range(kinds // 2):
        lhs = jnp.where(left, classes[2 * pair], classes[2 * pair + 1])
        rhs = jnp.concatenate([trans_leaf[2 * pair], trans_leaf[2 * pair + 1]], axis=0)
        box = box + own(lhs, rhs)
    up = own(box, trans_dev[dev_trans[0]])
    both = jnp.concatenate([box, up], axis=1)
    sums[...] = both
    high = both.astype(BF16)
    send_first[margin, :r] = high
    send_first[margin, r:] = (both - high.astype(F32)).astype(BF16)

    def fill(first_from, second_from):
        for leaf in range(margin):
            send_first[leaf, :r] = charges[first_from + leaf]
            send_first[leaf, r:] = moments[first_from + leaf]
            send_second[leaf, :r] = charges[second_from + leaf]
            send_second[leaf, r:] = moments[second_from + leaf]

    @pl.when(even)
    def _():
        fill(margin, 0)

    @pl.when(jnp.logical_not(even))
    def _():
        fill(0, margin)

    copies[6].wait()


def table_kernel(chunk, count, table, blocks, out, buffer, sems):
    half, kinds = table.shape[1], table.shape[3]
    live = count[0]
    copies = [
        pltpu.make_async_copy(
            blocks.at[pl.ds(i * chunk, chunk)], buffer.at[pl.ds(i * chunk, chunk)], sems.at[i]
        )
        for i in range(blocks.shape[0] // chunk)
    ]
    for i, copy in enumerate(copies):

        @pl.when(i * chunk < live)
        def _():
            copy.start()

    def step(row, carry):
        stacked = jnp.concatenate([table[0, row], table[1, row]], axis=0)
        for start in range(0, kinds, 128):
            width = min(128, kinds - start)
            out[pl.ds(start * half + row, width, stride=half), :] = stacked[
                :, start : start + width
            ].T
        return carry

    lax.fori_loop(0, half, step, 0, unroll=8)
    for i, copy in enumerate(copies):

        @pl.when(i * chunk < live)
        def _():
            copy.wait()


def halo_places(leaves):
    margin = leaves // 2
    even = lax.rem(lax.axis_index("dev"), 2) == 0
    return jnp.where(even, margin + leaves, 0), jnp.where(even, 0, margin + leaves)


def first_leaf(leaves):
    return (lax.axis_index("grp") * lax.axis_size("dev") + lax.axis_index("dev")) * leaves


def near_kernel(
    chunk, targets, sources, count, charges, first, second, blocks, out, window, total
):
    slots = blocks.shape[0]
    leaves, r, panels = charges.shape
    margin = leaves // 2
    live = count[0]
    leaf_start = first_leaf(leaves)
    first_at, second_at = halo_places(leaves)
    window[pl.ds(margin, leaves)] = charges[...]
    window[pl.ds(first_at, margin)] = first[:margin, :r]
    window[pl.ds(second_at, margin)] = second[:, :r]
    total[...] = jnp.zeros_like(total)

    def picked(slot):
        return window[sources[slot] - leaf_start + margin]

    def step(index, carry):
        base = index * chunk
        products = []
        for u in range(0, chunk, 2):
            both = lax.dot_general(
                jnp.concatenate([picked(base + u), picked(base + u + 1)], axis=0),
                blocks[pl.ds(base + u, 2)].reshape(2 * panels, panels),
                NT, preferred_element_type=F32,
            )
            products += [both[:r, :panels], both[r:, panels:]]
        for u in range(chunk):
            slot = base + u
            row = jnp.where(slot < live, targets[slot] - leaf_start, leaves)
            total[row] = total[row] + products[u]
        return carry

    lax.fori_loop(0, (live + chunk - 1) // chunk, step, 0)
    out[...] = total[:leaves]


def couple(table, kind, half):
    return table[pl.ds(pl.multiple_of(kind * half, half), half), :]


def far_leaves(start, far, far_couple, spread, table, out):
    count, r, k = out.shape
    leaves = spread.shape[0] // 2
    nfar = far.shape[0]
    width, half = 2 * k, k // 2
    origin = first_leaf(leaves) - leaves // 2
    lane = lax.broadcasted_iota(jnp.int32, (4 * r, width), 1) // half
    results = []
    for leaf in range(start, start + count):
        lhs, rhs = [], []
        for quad in range(nfar // 4):
            picked = None
            tables = []
            for q in range(4):
                f = quad * 4 + q
                source = spread[far[f, leaf] - origin]
                picked = source if q == 0 else jnp.where(lane >= q, source, picked)
                tables.append(couple(table, far_couple[f, leaf], half))
            stacked = jnp.concatenate(tables, axis=0)
            high = stacked.astype(BF16)
            low = (stacked - high.astype(F32)).astype(BF16)
            lhs.append(picked)
            rhs.append(jnp.concatenate([high, low], axis=1))
        product = jnp.dot(
            jnp.concatenate(lhs, axis=1), jnp.concatenate(rhs, axis=0),
            preferred_element_type=F32,
        )
        product = product[: 2 * r] + product[2 * r :]
        out[leaf - start] = fold(product[:, :width] + product[:, width:])


def far_low_kernel(
    far, far_couple, moments, first, second, table, out, spread, window
):
    leaves, r, width = moments.shape
    margin = leaves // 2
    half = width // 4
    first_at, second_at = halo_places(leaves)
    window[pl.ds(margin, leaves)] = moments[...]
    window[pl.ds(first_at, margin)] = first[:margin, r:]
    window[pl.ds(second_at, margin)] = second[:, r:]
    row = lax.broadcasted_iota(jnp.int32, (width, 4 * width), 0)
    column = lax.broadcasted_iota(jnp.int32, (width, 4 * width), 1)
    copier = (row == (column // width) * half + lax.rem(column, half)).astype(BF16)
    piece = 8
    for start in range(0, 2 * leaves, piece):
        rows = window[start : start + piece].reshape(piece * r, width)
        copied = jnp.dot(rows, copier, preferred_element_type=F32).astype(BF16)
        for section in range(4):
            spread[start : start + piece, section * r : (section + 1) * r] = copied[
                :, section * width : (section + 1) * width
            ].reshape(piece, r, width)
    far_leaves(0, far, far_couple, spread, table, out)


def far_high_kernel(
    far, far_couple, dev_list, dev_couple, grp_couple, spread, table, boxes,
    out, listed_out, group_tables,
):
    _, r, k = out.shape
    half = k // 2
    group = lax.axis_index("grp")
    member = lax.axis_index("dev")
    far_leaves(out.shape[0], far, far_couple, spread, table, out)
    lhs, rhs = [], []
    for n in range(dev_list.shape[1]):
        place = jnp.bitwise_xor(dev_list[0, n] - group * lax.axis_size("dev"), member)
        lhs.append(halves(boxes[place][:, :k]))
        rhs.append(couple(table, dev_couple[0, n], half))
    listed_out[...] = fold(
        jnp.dot(
            jnp.concatenate(lhs, axis=1), jnp.concatenate(rhs, axis=0),
            precision=HIGHEST, preferred_element_type=F32,
        )
    )
    for other in range(1, grp_couple.shape[0]):
        group_tables[other - 1] = couple(
            table, grp_couple[group, jnp.bitwise_xor(group, other)], half
        )


def final_kernel(
    leaf_trans, dev_trans, near, far_low, far_high, listed, group_tables, groups, basis_t,
    trans_leaf, trans_dev, out, locals_,
):
    leaves = near.shape[0]
    own = functools.partial(lax.dot_general, precision=HIGHEST, preferred_element_type=F32)
    group_local = None
    for other in range(group_tables.shape[0]):
        term = fold(
            jnp.dot(
                halves(groups[other + 1]), group_tables[other],
                precision=HIGHEST, preferred_element_type=F32,
            )
        )
        group_local = term if other == 0 else group_local + term
    box_local = own(group_local, trans_dev[dev_trans[0]], NT) + listed[...]
    for kind in range(trans_leaf.shape[0]):
        locals_[kind] = own(box_local, trans_leaf[kind], NT)
    for leaf in range(leaves):
        far = far_low[leaf] if leaf < leaves // 2 else far_high[leaf - leaves // 2]
        leaf_local = (locals_[leaf_trans[leaf]] + far).astype(BF16)
        out[leaf] = near[leaf] + jnp.dot(
            leaf_local, basis_t[leaf], preferred_element_type=F32
        )


def swap(x, axis, distance):
    return lax.ppermute(x, axis, [(i, i ^ distance) for i in range(lax.axis_size(axis))])


def cost(us):
    return pl.CostEstimate(flops=0, bytes_accessed=us * 3 * MIB, transcendentals=0)


def params(mib):
    return pltpu.CompilerParams(vmem_limit_bytes=mib * MIB)


def local(
    charges,
    leaf_basis,
    near_blocks,
    near_target,
    near_source,
    near_count,
    leaf_far,
    leaf_far_couple,
    leaf_trans,
    dev_trans,
    dev_list,
    dev_couple,
    grp_couple,
    trans_leaf,
    trans_dev,
    couple_table,
):
    leaves, r, panels = charges.shape
    k = leaf_basis.shape[2]
    margin = leaves // 2
    slots = near_blocks.shape[0]
    kinds = couple_table.shape[0]
    half = k // 2
    per_group = lax.axis_size("dev")
    devices = per_group * lax.axis_size("grp")
    basis_t = jnp.swapaxes(leaf_basis, 1, 2)
    shape = jax.ShapeDtypeStruct

    moments, send_first, send_second, sums, own_charges, basis, leaf_maps, dev_maps, raw = (
        pl.pallas_call(
            moment_kernel,
            out_shape=(
                shape((leaves, r, 2 * k), BF16),
                shape((margin + 1, 2 * r, panels), BF16),
                shape((margin, 2 * r, panels), BF16),
                shape((r, 2 * k), F32),
                shape(charges.shape, BF16),
                shape(basis_t.shape, BF16),
                shape(trans_leaf.shape, F32),
                shape(trans_dev.shape, F32),
                shape((2, half, k, kinds), F32),
            ),
            in_specs=[HBM] * 7,
            out_specs=(VMEM,) * 9,
            scratch_shapes=[
                pltpu.SMEM(leaf_trans.shape, jnp.int32),
                pltpu.SMEM(dev_trans.shape, jnp.int32),
                pltpu.VMEM((trans_leaf.shape[0], r, 2 * k), F32),
                pltpu.SemaphoreType.DMA((7,)),
            ],
            compiler_params=params(24),
            name="moments",
        )(
            leaf_trans, dev_trans, charges, basis_t, trans_leaf, trans_dev,
            jnp.transpose(couple_table, (1, 2, 0)).reshape(2, half, k, kinds),
        )
    )

    first = swap(send_first, "dev", 1)
    partners = [(i, i + 1) for i in range(1, devices - 1, 2)] + [(0, devices - 1)]
    second = lax.ppermute(send_second, AXES, partners + [(j, i) for i, j in partners])

    chunk = slots // 5
    table, blocks = pl.pallas_call(
        functools.partial(table_kernel, chunk),
        out_shape=(shape((kinds * half, 2 * k), F32), shape(near_blocks.shape, BF16)),
        in_specs=[SMEM, VMEM, HBM],
        out_specs=(VMEM, VMEM),
        scratch_shapes=[pltpu.SemaphoreType.DMA((slots // chunk,))],
        compiler_params=params(24),
        cost_estimate=cost(3),
        name="table",
    )(near_count, raw, near_blocks)

    peer = first[margin, :r].astype(F32) + first[margin, r:].astype(F32)
    boxes = jnp.stack([sums, peer])
    boxes, table, blocks, first, second = lax.optimization_barrier(
        (boxes, table, blocks, first, second)
    )
    boxes_next = jnp.concatenate([boxes, swap(boxes, "dev", 2)])

    near = pl.pallas_call(
        functools.partial(near_kernel, chunk),
        out_shape=shape((leaves, r, panels), F32),
        in_specs=[SMEM, SMEM, SMEM, VMEM, VMEM, VMEM, VMEM],
        out_specs=VMEM,
        scratch_shapes=[
            pltpu.VMEM((2 * leaves, r, panels), BF16),
            pltpu.VMEM((leaves + 1, r, panels), F32),
        ],
        compiler_params=params(16),
        cost_estimate=cost(3),
        name="near",
    )(near_target, near_source, near_count, own_charges, first, second, blocks)
    boxes, near, table = lax.optimization_barrier((boxes_next, near, table))

    far_list, far_kinds = leaf_far.T, leaf_far_couple.T
    boxes_next = boxes
    for distance in [4 << i for i in range((per_group // 4).bit_length() - 1)]:
        boxes_next = jnp.concatenate([boxes_next, swap(boxes_next, "dev", distance)])
    far_low, spread = pl.pallas_call(
        far_low_kernel,
        out_shape=(shape((margin, r, k), F32), shape((2 * leaves, 4 * r, 2 * k), BF16)),
        in_specs=[SMEM] * 2 + [VMEM] * 4,
        out_specs=(VMEM, VMEM),
        scratch_shapes=[pltpu.VMEM((2 * leaves, r, 2 * k), BF16)],
        compiler_params=params(16),
        cost_estimate=cost(3),
        name="far_low",
    )(far_list, far_kinds, moments, first, second, table)
    boxes, far_low, spread, table = lax.optimization_barrier(
        (boxes_next, far_low, spread, table)
    )

    groups = jnp.sum(boxes[:, :, k:], axis=0)[None]
    for distance in [1 << i for i in range(lax.axis_size("grp").bit_length() - 1)]:
        groups = jnp.concatenate([groups, swap(groups, "grp", distance)])
    far_high, listed, group_tables = pl.pallas_call(
        far_high_kernel,
        out_shape=(
            shape((leaves - margin, r, k), F32),
            shape((r, k), F32),
            shape((lax.axis_size("grp") - 1, half, 2 * k), F32),
        ),
        in_specs=[SMEM] * 5 + [VMEM] * 3,
        out_specs=(VMEM, VMEM, VMEM),
        compiler_params=params(16),
        cost_estimate=cost(3),
        name="far_high",
    )(far_list, far_kinds, dev_list, dev_couple, grp_couple, spread, table, boxes)

    return pl.pallas_call(
        final_kernel,
        out_shape=shape((leaves, r, panels), F32),
        in_specs=[SMEM, SMEM] + [VMEM] * 9,
        out_specs=VMEM,
        scratch_shapes=[pltpu.VMEM((trans_leaf.shape[0], r, k), F32)],
        compiler_params=params(16),
        name="final",
    )(
        leaf_trans, dev_trans, near, far_low, far_high, listed, group_tables, groups, basis,
        leaf_maps, dev_maps,
    )


def solution(mesh):
    leaf = P(AXES)
    return jax.shard_map(
        local,
        mesh=mesh,
        in_specs=(leaf,) * 12 + (P(),) * 4,
        out_specs=leaf,
        check_vma=False,
    )
```

```python
import functools

import jax
import jax.numpy as jnp
from jax import lax
from jax.experimental import pallas as pl
from jax.experimental.pallas import tpu as pltpu
from jax.sharding import PartitionSpec as P

F32 = jnp.float32
BF16 = jnp.bfloat16
NT = (((1,), (1,)), ((), ()))
AXES = ("grp", "dev")
VMEM = pl.BlockSpec(memory_space=pltpu.VMEM)
SMEM = pl.BlockSpec(memory_space=pltpu.SMEM)
HBM = pl.BlockSpec(memory_space=pltpu.HBM)
MIB = 2**20


def halves(x):
    half = x.shape[1] // 2
    return jnp.concatenate([x[:, :half], x[:, half:]], axis=0)


def fold(product):
    r, j = product.shape[0] // 2, product.shape[1] // 2
    return product[:r, :j] + product[r:, j:]


def split(x):
    high = x.astype(BF16)
    return high, (x - high.astype(F32)).astype(BF16)


def dot3(a, b, dims=(((1,), (0,)), ((), ()))):
    (a_high, a_low), (b_high, b_low) = split(a), split(b)
    both = lax.dot_general(
        jnp.concatenate([a_high, a_low], axis=0), b_high, dims, preferred_element_type=F32
    )
    rest = lax.dot_general(a_high, b_low, dims, preferred_element_type=F32)
    return both[: a.shape[0]] + both[a.shape[0] :] + rest


def moment_kernel(
    leaf_trans_hbm, dev_trans_hbm, charges_hbm, basis_hbm, trans_leaf_hbm, trans_dev_hbm, table_hbm,
    moments, send_first, send_second, sums, leaf_trans, dev_trans, charges, basis_t,
    trans_leaf, trans_dev, table, classes, sems,
):
    moves = [
        (charges_hbm, charges), (basis_hbm, basis_t), (leaf_trans_hbm, leaf_trans),
        (trans_leaf_hbm, trans_leaf), (dev_trans_hbm, dev_trans), (trans_dev_hbm, trans_dev),
        (table_hbm, table),
    ]
    copies = [
        pltpu.make_async_copy(source, target, sems.at[i])
        for i, (source, target) in enumerate(moves)
    ]
    for copy in copies:
        copy.start()
    leaves, r, _ = charges.shape
    k = basis_t.shape[1]
    margin = leaves // 2
    kinds = trans_leaf.shape[0]
    even = lax.rem(lax.axis_index("dev"), 2) == 0
    left = lax.broadcasted_iota(jnp.int32, (r, 2 * k), 1) < k
    classes[...] = jnp.zeros_like(classes)
    for copy in copies[:3]:
        copy.wait()
    for leaf in range(leaves):
        basis = basis_t[leaf]
        twice = lax.dot_general(
            charges[leaf], jnp.concatenate([basis, basis], axis=0), NT,
            preferred_element_type=F32,
        )
        kind = leaf_trans[leaf]
        classes[kind] = classes[kind] + twice
        high = twice.astype(BF16).astype(F32)
        moments[leaf] = jnp.where(left, high, twice - high).astype(BF16)
    for copy in copies[3:6]:
        copy.wait()
    lhs = [
        jnp.where(left, classes[kind], classes[kind + 1]) for kind in range(0, kinds, 2)
    ]
    box = dot3(jnp.concatenate(lhs, axis=1), trans_leaf[...].reshape(kinds * k, k))
    up = dot3(box, trans_dev[dev_trans[0]])
    both = jnp.concatenate([box, up], axis=1)
    sums[...] = both
    high = both.astype(BF16)
    send_first[margin, :r] = high
    send_first[margin, r:] = (both - high.astype(F32)).astype(BF16)

    def fill(first_from, second_from):
        for leaf in range(margin):
            send_first[leaf, :r] = charges[first_from + leaf]
            send_first[leaf, r:] = moments[first_from + leaf]
            send_second[leaf, :r] = charges[second_from + leaf]
            send_second[leaf, r:] = moments[second_from + leaf]

    @pl.when(even)
    def _():
        fill(margin, 0)

    @pl.when(jnp.logical_not(even))
    def _():
        fill(0, margin)

    copies[6].wait()


def relayout(table, row, out, count):
    kinds = table.shape[3]
    stacked = jnp.concatenate([table[0, row], table[1, row]], axis=0)
    for start in range(0, kinds, 128):
        width = min(128, kinds - start)
        out[pl.ds(start * count + lax.rem(row, count), width, stride=count), :] = stacked[
            :, start : start + width
        ].T


def table_kernel(table, blocks_hbm, out, blocks, sem):
    copy = pltpu.make_async_copy(blocks_hbm, blocks, sem)
    copy.start()
    rows = table.shape[1] // 2

    def step(row, carry):
        relayout(table, row, out, rows)
        return carry

    lax.fori_loop(0, rows, step, 0, unroll=8)
    copy.wait()


def halo_places(leaves):
    margin = leaves // 2
    even = lax.rem(lax.axis_index("dev"), 2) == 0
    return jnp.where(even, margin + leaves, 0), jnp.where(even, 0, margin + leaves)


def first_leaf(leaves):
    return (lax.axis_index("grp") * lax.axis_size("dev") + lax.axis_index("dev")) * leaves


def near_kernel(
    steps, targets, sources, count, charges, first, second, blocks, table, out, table_out,
    window, total,
):
    chunk = blocks.shape[0] // steps
    leaves, r, panels = charges.shape
    margin = leaves // 2
    rows = table.shape[1] // 2
    live = count[0]
    leaf_start = first_leaf(leaves)
    first_at, second_at = halo_places(leaves)
    window[pl.ds(margin, leaves)] = charges[...]
    window[pl.ds(first_at, margin)] = first[:margin, :r]
    window[pl.ds(second_at, margin)] = second[:, :r]
    total[...] = jnp.zeros_like(total)

    def picked(slot):
        return window[sources[slot] - leaf_start + margin]

    def step(index, carry):
        base = index * chunk
        products = []
        for u in range(0, chunk, 2):
            both = lax.dot_general(
                jnp.concatenate([picked(base + u), picked(base + u + 1)], axis=0),
                blocks[pl.ds(base + u, 2)].reshape(2 * panels, panels),
                NT, preferred_element_type=F32,
            )
            products += [both[:r, :panels], both[r:, panels:]]
        for u in range(rows // steps):
            relayout(table, rows + index * (rows // steps) + u, table_out, rows)
        for u in range(chunk):
            slot = base + u
            row = jnp.where(slot < live, targets[slot] - leaf_start, leaves)
            total[row] = total[row] + products[u]
        return carry

    lax.fori_loop(0, steps, step, 0)
    out[...] = total[:leaves]


def couple(tables, kind):
    return jnp.concatenate([table[kind] for table in tables], axis=0)


def far_kernel(
    far, far_couple, dev_list, dev_couple, grp_couple, moments, first, second, table_low,
    table_high, boxes, out, listed_out, group_tables, window, spread,
):
    leaves, r, width = moments.shape
    margin = leaves // 2
    k, half = width // 2, width // 4
    nfar = far.shape[0]
    tables = (table_low, table_high)
    group = lax.axis_index("grp")
    member = lax.axis_index("dev")
    origin = first_leaf(leaves) - margin
    first_at, second_at = halo_places(leaves)
    window[pl.ds(margin, leaves)] = moments[...]
    window[pl.ds(first_at, margin)] = first[:margin, r:]
    window[pl.ds(second_at, margin)] = second[:, r:]
    row = lax.broadcasted_iota(jnp.int32, (width, 4 * width), 0)
    column = lax.broadcasted_iota(jnp.int32, (width, 4 * width), 1)
    copier = (row == (column // width) * half + lax.rem(column, half)).astype(BF16)
    piece = 8
    for start in range(0, 2 * leaves, piece):
        rows = window[start : start + piece].reshape(piece * r, width)
        copied = jnp.dot(rows, copier, preferred_element_type=F32).astype(BF16)
        for section in range(4):
            spread[start : start + piece, section * r : (section + 1) * r] = copied[
                :, section * width : (section + 1) * width
            ].reshape(piece, r, width)
    lane = lax.broadcasted_iota(jnp.int32, (4 * r, width), 1) // half
    for leaf in range(leaves):
        lhs, rhs = [], []
        for quad in range(nfar // 4):
            picked = None
            taken = []
            for q in range(4):
                f = quad * 4 + q
                source = spread[far[f, leaf] - origin]
                picked = source if q == 0 else jnp.where(lane >= q, source, picked)
                taken.append(couple(tables, far_couple[f, leaf]))
            lhs.append(picked)
            rhs.append(jnp.concatenate(split(jnp.concatenate(taken, axis=0)), axis=1))
        product = jnp.dot(
            jnp.concatenate(lhs, axis=1), jnp.concatenate(rhs, axis=0),
            preferred_element_type=F32,
        )
        product = product[: 2 * r] + product[2 * r :]
        out[leaf] = fold(product[:, :width] + product[:, width:])
    lhs, rhs = [], []
    for n in range(dev_list.shape[1]):
        place = jnp.bitwise_xor(dev_list[0, n] - group * lax.axis_size("dev"), member)
        lhs.append(halves(boxes[place][:, :k]))
        rhs.append(couple(tables, dev_couple[0, n]))
    listed_out[...] = fold(dot3(jnp.concatenate(lhs, axis=1), jnp.concatenate(rhs, axis=0)))
    for other in range(1, grp_couple.shape[0]):
        group_tables[(other - 1) * half : other * half] = couple(
            tables, grp_couple[group, jnp.bitwise_xor(group, other)]
        )


def final_kernel(
    steps, leaf_trans, dev_trans, near, far, listed, group_tables, groups, basis_t,
    trans_leaf, trans_dev, out_hbm, out, locals_, sems,
):
    leaves = near.shape[0]
    kinds, k, _ = trans_leaf.shape
    lhs = [halves(groups[other]) for other in range(groups.shape[0])]
    group_local = fold(dot3(jnp.concatenate(lhs, axis=1), group_tables[...]))
    box_local = dot3(group_local, trans_dev[dev_trans[0]], NT) + listed[...]
    by_kind = dot3(box_local, trans_leaf[...].reshape(kinds * k, k), NT)
    for kind in range(kinds):
        locals_[kind] = by_kind[:, kind * k : (kind + 1) * k]
    size = leaves // steps
    copies = []
    for i in range(steps):
        for leaf in range(i * size, (i + 1) * size):
            leaf_local = (locals_[leaf_trans[leaf]] + far[leaf]).astype(BF16)
            out[leaf] = near[leaf] + jnp.dot(
                leaf_local, basis_t[leaf], preferred_element_type=F32
            )
        piece = pl.ds(i * size, size)
        copies.append(pltpu.make_async_copy(out.at[piece], out_hbm.at[piece], sems.at[i]))
        copies[-1].start()
    for copy in copies:
        copy.wait()


def swap(x, axis, distance):
    return lax.ppermute(x, axis, [(i, i ^ distance) for i in range(lax.axis_size(axis))])


def cost(us):
    return pl.CostEstimate(flops=0, bytes_accessed=us * 3 * MIB, transcendentals=0)


def params(mib):
    return pltpu.CompilerParams(vmem_limit_bytes=mib * MIB)


def local(
    charges,
    leaf_basis,
    near_blocks,
    near_target,
    near_source,
    near_count,
    leaf_far,
    leaf_far_couple,
    leaf_trans,
    dev_trans,
    dev_list,
    dev_couple,
    grp_couple,
    trans_leaf,
    trans_dev,
    couple_table,
):
    leaves, r, panels = charges.shape
    k = leaf_basis.shape[2]
    margin = leaves // 2
    slots = near_blocks.shape[0]
    kinds = couple_table.shape[0]
    half = k // 2
    per_group = lax.axis_size("dev")
    devices = per_group * lax.axis_size("grp")
    basis_t = jnp.swapaxes(leaf_basis, 1, 2)
    shape = jax.ShapeDtypeStruct

    (
        moments, send_first, send_second, sums, leaf_kinds, dev_kind, own_charges, basis,
        leaf_maps, dev_maps, raw,
    ) = (
        pl.pallas_call(
            moment_kernel,
            out_shape=(
                shape((leaves, r, 2 * k), BF16),
                shape((margin + 1, 2 * r, panels), BF16),
                shape((margin, 2 * r, panels), BF16),
                shape((r, 2 * k), F32),
                shape(leaf_trans.shape, jnp.int32),
                shape(dev_trans.shape, jnp.int32),
                shape(charges.shape, BF16),
                shape(basis_t.shape, BF16),
                shape(trans_leaf.shape, F32),
                shape(trans_dev.shape, F32),
                shape((2, half, k, kinds), F32),
            ),
            in_specs=[HBM] * 7,
            out_specs=(VMEM,) * 4 + (SMEM,) * 2 + (VMEM,) * 5,
            scratch_shapes=[
                pltpu.VMEM((trans_leaf.shape[0], r, 2 * k), F32),
                pltpu.SemaphoreType.DMA((7,)),
            ],
            compiler_params=params(24),
            name="moments",
        )(
            pltpu.with_memory_space_constraint(leaf_trans, pltpu.HBM),
            dev_trans,
            pltpu.with_memory_space_constraint(charges, pltpu.HBM),
            pltpu.with_memory_space_constraint(basis_t, pltpu.HBM),
            pltpu.with_memory_space_constraint(trans_leaf, pltpu.HBM),
            pltpu.with_memory_space_constraint(trans_dev, pltpu.HBM),
            pltpu.with_memory_space_constraint(jnp.transpose(couple_table, (1, 2, 0)).reshape(2, half, k, kinds), pltpu.HBM),
        )
    )

    first = swap(send_first, "dev", 1)
    partners = [(i, i + 1) for i in range(1, devices - 1, 2)] + [(0, devices - 1)]
    second = lax.ppermute(send_second, AXES, partners + [(j, i) for i, j in partners])

    table_low, blocks = pl.pallas_call(
        table_kernel,
        out_shape=(
            shape((kinds * half // 2, 2 * k), F32),
            shape(near_blocks.shape, BF16),
        ),
        in_specs=[VMEM, HBM],
        out_specs=(VMEM, VMEM),
        scratch_shapes=[pltpu.SemaphoreType.DMA],
        compiler_params=params(24),
        cost_estimate=cost(3),
        name="table",
    )(raw, pltpu.with_memory_space_constraint(near_blocks, pltpu.HBM))

    peer = first[margin, :r].astype(F32) + first[margin, r:].astype(F32)
    pair = jnp.stack([sums, peer])
    pair, table_low, blocks, first, second = lax.optimization_barrier(
        (pair, table_low, blocks, first, second)
    )
    boxes = [pair] + [swap(pair, "dev", distance) for distance in range(2, per_group, 2)]

    steps = 4
    near, table_high = pl.pallas_call(
        functools.partial(near_kernel, steps),
        out_shape=(
            shape((leaves, r, panels), F32),
            shape((kinds * half // 2, 2 * k), F32),
        ),
        in_specs=[SMEM, SMEM, SMEM, VMEM, VMEM, VMEM, VMEM, VMEM],
        out_specs=(VMEM, VMEM),
        scratch_shapes=[
            pltpu.VMEM((2 * leaves, r, panels), BF16),
            pltpu.VMEM((leaves + 1, r, panels), F32),
        ],
        compiler_params=params(16),
        cost_estimate=cost(3),
        name="near",
    )(near_target, near_source, near_count, own_charges, first, second, blocks, raw)
    boxes = jnp.concatenate(boxes)
    boxes, near, table_high = lax.optimization_barrier((boxes, near, table_high))

    group_moment = jnp.sum(boxes[:, :, k:], axis=0)
    groups = [
        swap(group_moment, "grp", distance) for distance in range(1, lax.axis_size("grp"))
    ]
    tables = [x.reshape(kinds, half // 2, 2 * k) for x in (table_low, table_high)]
    far, listed, group_tables = pl.pallas_call(
        far_kernel,
        out_shape=(
            shape((leaves, r, k), F32),
            shape((r, k), F32),
            shape((len(groups) * half, 2 * k), F32),
        ),
        in_specs=[SMEM] * 5 + [VMEM] * 6,
        out_specs=(VMEM, VMEM, VMEM),
        scratch_shapes=[
            pltpu.VMEM((2 * leaves, r, 2 * k), BF16),
            pltpu.VMEM((2 * leaves, 4 * r, 2 * k), BF16),
        ],
        compiler_params=params(16),
        cost_estimate=cost(3),
        name="far",
    )(
        leaf_far.T, leaf_far_couple.T, dev_list, dev_couple, grp_couple, moments, first,
        second, *tables, boxes,
    )

    return pl.pallas_call(
        functools.partial(final_kernel, steps),
        out_shape=shape((leaves, r, panels), F32),
        in_specs=[SMEM, SMEM] + [VMEM] * 8,
        out_specs=HBM,
        scratch_shapes=[
            pltpu.VMEM((leaves, r, panels), F32),
            pltpu.VMEM((trans_leaf.shape[0], r, k), F32),
            pltpu.SemaphoreType.DMA((steps,)),
        ],
        compiler_params=params(16),
        name="final",
    )(
        leaf_kinds, dev_kind, near, far, listed, group_tables, jnp.stack(groups), basis,
        leaf_maps, dev_maps,
    )


def solution(mesh):
    leaf = P(AXES)
    return jax.shard_map(
        local,
        mesh=mesh,
        in_specs=(leaf,) * 12 + (P(),) * 4,
        out_specs=leaf,
        check_vma=False,
    )
```

```python
import functools

import jax
import jax.numpy as jnp
from jax import lax
from jax.experimental import pallas as pl
from jax.experimental.pallas import tpu as pltpu
from jax.sharding import PartitionSpec as P

F32 = jnp.float32
BF16 = jnp.bfloat16
NT = (((1,), (1,)), ((), ()))
AXES = ("grp", "dev")
VMEM = pl.BlockSpec(memory_space=pltpu.VMEM)
SMEM = pl.BlockSpec(memory_space=pltpu.SMEM)
HBM = pl.BlockSpec(memory_space=pltpu.HBM)
MIB = 2**20


def halves(x):
    half = x.shape[1] // 2
    return jnp.concatenate([x[:, :half], x[:, half:]], axis=0)


def fold(product):
    r, j = product.shape[0] // 2, product.shape[1] // 2
    return product[:r, :j] + product[r:, j:]


def split(x):
    high = x.astype(BF16)
    return high, (x - high.astype(F32)).astype(BF16)


def dot3(a, b, dims=(((1,), (0,)), ((), ()))):
    (a_high, a_low), (b_high, b_low) = split(a), split(b)
    both = lax.dot_general(
        jnp.concatenate([a_high, a_low], axis=0), b_high, dims, preferred_element_type=F32
    )
    rest = lax.dot_general(a_high, b_low, dims, preferred_element_type=F32)
    return both[: a.shape[0]] + both[a.shape[0] :] + rest


def moment_kernel(
    leaf_trans_hbm, dev_trans, charges_hbm, basis_hbm, trans_leaf_hbm, trans_dev_hbm, table_hbm,
    moments, send_first, send_second, sums, leaf_trans, dev_trans_out, charges, basis_t,
    trans_leaf, trans_dev, table, classes, sems,
):
    moves = [
        (charges_hbm, charges), (basis_hbm, basis_t), (leaf_trans_hbm, leaf_trans),
        (trans_leaf_hbm, trans_leaf), (trans_dev_hbm, trans_dev),
        (table_hbm, table),
    ]
    copies = [
        pltpu.make_async_copy(source, target, sems.at[i])
        for i, (source, target) in enumerate(moves)
    ]
    for copy in copies:
        copy.start()
    leaves, r, _ = charges.shape
    k = basis_t.shape[1]
    margin = leaves // 2
    kinds = trans_leaf.shape[0]
    even = lax.rem(lax.axis_index("dev"), 2) == 0
    left = lax.broadcasted_iota(jnp.int32, (r, 2 * k), 1) < k
    classes[...] = jnp.zeros_like(classes)
    for copy in copies[:3]:
        copy.wait()
    for leaf in range(leaves):
        basis = basis_t[leaf]
        twice = lax.dot_general(
            charges[leaf], jnp.concatenate([basis, basis], axis=0), NT,
            preferred_element_type=F32,
        )
        kind = leaf_trans[leaf]
        classes[kind] = classes[kind] + twice
        high = twice.astype(BF16).astype(F32)
        moments[leaf] = jnp.where(left, high, twice - high).astype(BF16)
    for copy in copies[3:5]:
        copy.wait()
    lhs = [
        jnp.where(left, classes[kind], classes[kind + 1]) for kind in range(0, kinds, 2)
    ]
    box = dot3(jnp.concatenate(lhs, axis=1), trans_leaf[...].reshape(kinds * k, k))
    dev_trans_out[0] = dev_trans[0]
    up = dot3(box, trans_dev[dev_trans[0]])
    both = jnp.concatenate([box, up], axis=1)
    sums[...] = both

    def fill(first_from, second_from):
        for leaf in range(margin):
            send_first[leaf, :r] = charges[first_from + leaf]
            send_first[leaf, r:] = moments[first_from + leaf]
            send_second[leaf, :r] = charges[second_from + leaf]
            send_second[leaf, r:] = moments[second_from + leaf]

    @pl.when(even)
    def _():
        fill(margin, 0)

    @pl.when(jnp.logical_not(even))
    def _():
        fill(0, margin)

    copies[5].wait()


def relayout(table, row, out, place, count):
    kinds = table.shape[3]
    stacked = jnp.concatenate([table[0, row], table[1, row]], axis=0)
    for start in range(0, kinds, 128):
        width = min(128, kinds - start)
        out[pl.ds(start * count + place, width, stride=count), :] = stacked[
            :, start : start + width
        ].T


def relayout_rows(table, out, begin, rows):
    def step(place, carry):
        relayout(table, begin + place, out, place, rows)
        return carry

    lax.fori_loop(0, rows, step, 0, unroll=8)


def table_kernel(rows, count, table, out, count_out):
    count_out[0] = count[0]
    relayout_rows(table, out, 0, rows)


def halo_places(leaves):
    margin = leaves // 2
    even = lax.rem(lax.axis_index("dev"), 2) == 0
    return jnp.where(even, margin + leaves, 0), jnp.where(even, 0, margin + leaves)


def first_leaf(leaves):
    return (lax.axis_index("grp") * lax.axis_size("dev") + lax.axis_index("dev")) * leaves


def near_kernel(
    steps, begin, rows, targets, sources, count, charges, first, second, blocks, table, out, table_out,
    window, total,
):
    chunk = blocks.shape[0] // steps
    leaves, r, panels = charges.shape
    margin = leaves // 2
    live = count[0]
    leaf_start = first_leaf(leaves)
    first_at, second_at = halo_places(leaves)
    window[pl.ds(margin, leaves)] = charges[...]
    window[pl.ds(first_at, margin)] = first[:margin, :r]
    window[pl.ds(second_at, margin)] = second[:, :r]
    total[...] = jnp.zeros_like(total)

    def picked(slot):
        return window[sources[slot] - leaf_start + margin]

    def step(index, carry):
        base = index * chunk
        products = []
        for u in range(0, chunk, 2):
            both = lax.dot_general(
                jnp.concatenate([picked(base + u), picked(base + u + 1)], axis=0),
                blocks[pl.ds(base + u, 2)].reshape(2 * panels, panels),
                NT, preferred_element_type=F32,
            )
            products += [both[:r, :panels], both[r:, panels:]]
        for u in range(rows // steps):
            place = index * (rows // steps) + u
            relayout(table, begin + place, table_out, place, rows)
        for u in range(chunk):
            slot = base + u
            row = jnp.where(slot < live, targets[slot] - leaf_start, leaves)
            total[row] = total[row] + products[u]
        return carry

    lax.fori_loop(0, steps, step, 0)
    out[...] = total[:leaves]


def couple(tables, kind):
    return jnp.concatenate([table[kind] for table in tables], axis=0)


def far_kernel(
    parts, far, far_couple, dev_couple, grp_couple, moments, first, second, *rest
):
    tables = rest[:parts]
    out, box_tables, window, spread = rest[parts:]
    leaves, r, width = moments.shape
    margin = leaves // 2
    k, half = width // 2, width // 4
    nfar = far.shape[0]
    group = lax.axis_index("grp")
    origin = first_leaf(leaves) - margin
    first_at, second_at = halo_places(leaves)
    window[pl.ds(margin, leaves)] = moments[...]
    window[pl.ds(first_at, margin)] = first[:margin, r:]
    window[pl.ds(second_at, margin)] = second[:, r:]
    row = lax.broadcasted_iota(jnp.int32, (width, 4 * width), 0)
    column = lax.broadcasted_iota(jnp.int32, (width, 4 * width), 1)
    copier = (row == (column // width) * half + lax.rem(column, half)).astype(BF16)
    piece = 8
    for start in range(0, 2 * leaves, piece):
        rows = window[start : start + piece].reshape(piece * r, width)
        copied = jnp.dot(rows, copier, preferred_element_type=F32).astype(BF16)
        for section in range(4):
            spread[start : start + piece, section * r : (section + 1) * r] = copied[
                :, section * width : (section + 1) * width
            ].reshape(piece, r, width)
    lane = lax.broadcasted_iota(jnp.int32, (4 * r, width), 1) // half
    for leaf in range(leaves):
        lhs, rhs = [], []
        for quad in range(nfar // 4):
            picked = None
            taken = []
            for q in range(4):
                f = quad * 4 + q
                source = spread[far[f, leaf] - origin]
                picked = source if q == 0 else jnp.where(lane >= q, source, picked)
                taken.append(couple(tables, far_couple[f, leaf]))
            lhs.append(picked)
            rhs.append(jnp.concatenate(split(jnp.concatenate(taken, axis=0)), axis=1))
        product = jnp.dot(
            jnp.concatenate(lhs, axis=1), jnp.concatenate(rhs, axis=0),
            preferred_element_type=F32,
        )
        product = product[: 2 * r] + product[2 * r :]
        out[leaf] = fold(product[:, :width] + product[:, width:])
    wanted = [
        grp_couple[group, jnp.bitwise_xor(group, other)]
        for other in range(1, grp_couple.shape[0])
    ] + [dev_couple[0, n] for n in range(dev_couple.shape[1])]
    for i, kind in enumerate(wanted):
        box_tables[i * half : (i + 1) * half] = couple(tables, kind)


def final_kernel(
    steps, leaf_trans, dev_trans, dev_list, near, far, box_tables, boxes, groups, basis_t,
    trans_leaf, trans_dev, out_hbm, out, locals_, sems,
):
    leaves = near.shape[0]
    kinds, k, _ = trans_leaf.shape
    others = groups.shape[0] - 1
    group = lax.axis_index("grp")
    member = lax.axis_index("dev")
    split_at = others * (k // 2)
    lhs = [halves(groups[other + 1]) for other in range(others)]
    group_local = fold(dot3(jnp.concatenate(lhs, axis=1), box_tables[:split_at]))
    lhs = []
    for n in range(dev_list.shape[1]):
        place = jnp.bitwise_xor(dev_list[0, n] - group * lax.axis_size("dev"), member)
        lhs.append(halves(boxes[place]))
    listed = fold(dot3(jnp.concatenate(lhs, axis=1), box_tables[split_at:]))
    box_local = dot3(group_local, trans_dev[dev_trans[0]], NT) + listed
    by_kind = dot3(box_local, trans_leaf[...].reshape(kinds * k, k), NT)
    for kind in range(kinds):
        locals_[kind] = by_kind[:, kind * k : (kind + 1) * k]
    size = leaves // steps
    copies = []
    for i in range(steps):
        for leaf in range(i * size, (i + 1) * size):
            leaf_local = (locals_[leaf_trans[leaf]] + far[leaf]).astype(BF16)
            out[leaf] = near[leaf] + jnp.dot(
                leaf_local, basis_t[leaf], preferred_element_type=F32
            )
        piece = pl.ds(i * size, size)
        copies.append(pltpu.make_async_copy(out.at[piece], out_hbm.at[piece], sems.at[i]))
        copies[-1].start()
    for copy in copies:
        copy.wait()


def swap(x, axis, distance):
    return lax.ppermute(x, axis, [(i, i ^ distance) for i in range(lax.axis_size(axis))])


def cost(us):
    return pl.CostEstimate(flops=0, bytes_accessed=us * 3 * MIB, transcendentals=0)


def params(mib):
    return pltpu.CompilerParams(vmem_limit_bytes=mib * MIB)


def local(
    charges,
    leaf_basis,
    near_blocks,
    near_target,
    near_source,
    near_count,
    leaf_far,
    leaf_far_couple,
    leaf_trans,
    dev_trans,
    dev_list,
    dev_couple,
    grp_couple,
    trans_leaf,
    trans_dev,
    couple_table,
):
    leaves, r, panels = charges.shape
    k = leaf_basis.shape[2]
    margin = leaves // 2
    slots = near_blocks.shape[0]
    kinds = couple_table.shape[0]
    half = k // 2
    per_group = lax.axis_size("dev")
    devices = per_group * lax.axis_size("grp")
    basis_t = jnp.swapaxes(leaf_basis, 1, 2)
    shape = jax.ShapeDtypeStruct

    (
        moments, send_first, send_second, sums, leaf_kinds, dev_kind, own_charges, basis,
        leaf_maps, dev_maps, raw,
    ) = (
        pl.pallas_call(
            moment_kernel,
            out_shape=(
                shape((leaves, r, 2 * k), BF16),
                shape((margin, 2 * r, panels), BF16),
                shape((margin, 2 * r, panels), BF16),
                shape((r, 2 * k), F32),
                shape(leaf_trans.shape, jnp.int32),
                shape((8,), jnp.int32),
                shape(charges.shape, BF16),
                shape(basis_t.shape, BF16),
                shape(trans_leaf.shape, F32),
                shape(trans_dev.shape, F32),
                shape((2, half, k, kinds), F32),
            ),
            in_specs=[HBM, SMEM] + [HBM] * 5,
            out_specs=(VMEM,) * 4 + (SMEM,) * 2 + (VMEM,) * 5,
            scratch_shapes=[
                pltpu.VMEM((trans_leaf.shape[0], r, 2 * k), F32),
                pltpu.SemaphoreType.DMA((6,)),
            ],
            compiler_params=params(24),
            name="moments",
        )(
            pltpu.with_memory_space_constraint(leaf_trans, pltpu.HBM),
            dev_trans,
            pltpu.with_memory_space_constraint(charges, pltpu.HBM),
            pltpu.with_memory_space_constraint(basis_t, pltpu.HBM),
            pltpu.with_memory_space_constraint(trans_leaf, pltpu.HBM),
            pltpu.with_memory_space_constraint(trans_dev, pltpu.HBM),
            pltpu.with_memory_space_constraint(jnp.transpose(couple_table, (1, 2, 0)).reshape(2, half, k, kinds), pltpu.HBM),
        )
    )

    peer = swap(sums, "dev", 1)
    partners = [(i, i + 1) for i in range(1, devices - 1, 2)] + [(0, devices - 1)]
    second = lax.ppermute(send_second, AXES, partners + [(j, i) for i, j in partners])
    first = swap(send_first, "dev", 1)
    boxes = jnp.stack([sums[:, :k], peer[:, :k]])
    groups = (sums + peer)[None, :, k:]
    boxes, groups, raw = lax.optimization_barrier((boxes, groups, raw))

    groups = jnp.concatenate([groups, swap(groups, "grp", 1)])
    high_rows = half // 4
    low_rows = half - high_rows
    table_low, live = pl.pallas_call(
        functools.partial(table_kernel, low_rows),
        out_shape=(shape((kinds * low_rows, 2 * k), F32), shape((8,), jnp.int32)),
        in_specs=[SMEM, VMEM],
        out_specs=(VMEM, SMEM),
        compiler_params=params(16),
        cost_estimate=cost(3),
        name="table",
    )(near_count, raw)
    groups, table_low, live, first, second = lax.optimization_barrier(
        (groups, table_low, live, first, second)
    )
    for distance in [2 << i for i in range((lax.axis_size("grp") // 2).bit_length() - 1)]:
        groups = jnp.concatenate([groups, swap(groups, "grp", distance)])

    steps = 4

    def near_part():
        return pl.pallas_call(
            functools.partial(near_kernel, steps, low_rows, high_rows),
            out_shape=(
                shape((leaves, r, panels), F32),
                shape((kinds * high_rows, 2 * k), F32),
            ),
            in_specs=[SMEM, SMEM, SMEM, VMEM, VMEM, VMEM, VMEM, VMEM],
            out_specs=(VMEM, VMEM),
            scratch_shapes=[
                pltpu.VMEM((2 * leaves, r, panels), BF16),
                pltpu.VMEM((leaves + 1, r, panels), F32),
            ],
            compiler_params=params(16),
            cost_estimate=cost(3),
            name="near",
        )(
            near_target, near_source, live, own_charges, first, second,
            near_blocks, raw,
        )

    near, table_high = near_part()
    boxes, groups, near, table_high = lax.optimization_barrier((boxes, groups, near, table_high))
    parts = jnp.concatenate([boxes, groups])
    got = [swap(parts, "dev", distance) for distance in range(2, per_group, 2)]
    boxes = jnp.concatenate([boxes] + [part[:2] for part in got])
    groups = sum([part[2:] for part in got], start=groups)

    tables = [
        x.reshape(kinds, x.shape[0] // kinds, 2 * k) for x in (table_low, table_high)
    ]
    wanted = groups.shape[0] - 1 + dev_couple.shape[1]
    far, box_tables = pl.pallas_call(
        functools.partial(far_kernel, len(tables)),
        out_shape=(shape((leaves, r, k), F32), shape((wanted * half, 2 * k), F32)),
        in_specs=[SMEM] * 4 + [VMEM] * (3 + len(tables)),
        out_specs=(VMEM, VMEM),
        scratch_shapes=[
            pltpu.VMEM((2 * leaves, r, 2 * k), BF16),
            pltpu.VMEM((2 * leaves, 4 * r, 2 * k), BF16),
        ],
        compiler_params=params(16),
        cost_estimate=cost(3),
        name="far",
    )(
        leaf_far.T, leaf_far_couple.T, dev_couple, grp_couple, moments, first, second, *tables
    )

    return pl.pallas_call(
        functools.partial(final_kernel, steps),
        out_shape=shape((leaves, r, panels), F32),
        in_specs=[SMEM] * 3 + [VMEM] * 8,
        out_specs=HBM,
        scratch_shapes=[
            pltpu.VMEM((leaves, r, panels), F32),
            pltpu.VMEM((trans_leaf.shape[0], r, k), F32),
            pltpu.SemaphoreType.DMA((steps,)),
        ],
        compiler_params=params(16),
        name="final",
    )(
        leaf_kinds, dev_kind, dev_list, near, far, box_tables, boxes, groups, basis,
        leaf_maps, dev_maps,
    )


def solution(mesh):
    leaf = P(AXES)
    return jax.shard_map(
        local,
        mesh=mesh,
        in_specs=(leaf,) * 12 + (P(),) * 4,
        out_specs=leaf,
        check_vma=False,
    )
```

```python
import functools

import jax
import jax.numpy as jnp
from jax import lax
from jax.experimental import pallas as pl
from jax.experimental.pallas import tpu as pltpu
from jax.sharding import PartitionSpec as P

F32 = jnp.float32
BF16 = jnp.bfloat16
NT = (((1,), (1,)), ((), ()))
AXES = ("grp", "dev")
VMEM = pl.BlockSpec(memory_space=pltpu.VMEM)
SMEM = pl.BlockSpec(memory_space=pltpu.SMEM)
HBM = pl.BlockSpec(memory_space=pltpu.HBM)
MIB = 2**20


def halves(x):
    half = x.shape[1] // 2
    return jnp.concatenate([x[:, :half], x[:, half:]], axis=0)


def fold(product):
    r, j = product.shape[0] // 2, product.shape[1] // 2
    return product[:r, :j] + product[r:, j:]


def split(x):
    high = x.astype(BF16)
    return high, (x - high.astype(F32)).astype(BF16)


def dot3(a, b, dims=(((1,), (0,)), ((), ()))):
    (a_high, a_low), (b_high, b_low) = split(a), split(b)
    both = lax.dot_general(
        jnp.concatenate([a_high, a_low], axis=0), b_high, dims, preferred_element_type=F32
    )
    rest = lax.dot_general(a_high, b_low, dims, preferred_element_type=F32)
    return both[: a.shape[0]] + both[a.shape[0] :] + rest


def moment_kernel(
    leaf_trans_hbm, dev_trans, charges_hbm, basis_hbm, trans_leaf_hbm, trans_dev_hbm, table_hbm,
    moments, send_first, send_second, sums, leaf_trans, dev_trans_out, charges, basis_t,
    trans_leaf, trans_dev, table, classes, sems,
):
    moves = [
        (charges_hbm, charges), (basis_hbm, basis_t), (leaf_trans_hbm, leaf_trans),
        (trans_leaf_hbm, trans_leaf), (trans_dev_hbm, trans_dev),
        (table_hbm, table),
    ]
    copies = [
        pltpu.make_async_copy(source, target, sems.at[i])
        for i, (source, target) in enumerate(moves)
    ]
    for copy in copies:
        copy.start()
    leaves, r, _ = charges.shape
    k = basis_t.shape[1]
    margin = leaves // 2
    kinds = trans_leaf.shape[0]
    even = lax.rem(lax.axis_index("dev"), 2) == 0
    left = lax.broadcasted_iota(jnp.int32, (r, 2 * k), 1) < k
    classes[...] = jnp.zeros_like(classes)
    for copy in copies[:3]:
        copy.wait()
    for leaf in range(leaves):
        basis = basis_t[leaf]
        twice = lax.dot_general(
            charges[leaf], jnp.concatenate([basis, basis], axis=0), NT,
            preferred_element_type=F32,
        )
        kind = leaf_trans[leaf]
        classes[kind] = classes[kind] + twice
        high = twice.astype(BF16).astype(F32)
        moments[leaf] = jnp.where(left, high, twice - high).astype(BF16)
    for copy in copies[3:5]:
        copy.wait()
    lhs = [
        jnp.where(left, classes[kind], classes[kind + 1]) for kind in range(0, kinds, 2)
    ]
    box = dot3(jnp.concatenate(lhs, axis=1), trans_leaf[...].reshape(kinds * k, k))
    dev_trans_out[0] = dev_trans[0]
    up = dot3(box, trans_dev[dev_trans[0]])
    both = jnp.concatenate([box, up], axis=1)
    sums[...] = both

    def fill(first_from, second_from):
        for leaf in range(margin):
            send_first[leaf, :r] = charges[first_from + leaf]
            send_first[leaf, r:] = moments[first_from + leaf]
            send_second[leaf, :r] = charges[second_from + leaf]
            send_second[leaf, r:] = moments[second_from + leaf]

    @pl.when(even)
    def _():
        fill(margin, 0)

    @pl.when(jnp.logical_not(even))
    def _():
        fill(0, margin)

    copies[5].wait()


def relayout(table, row, out, place, count):
    kinds = table.shape[3]
    stacked = jnp.concatenate([table[0, row], table[1, row]], axis=0)
    for start in range(0, kinds, 128):
        width = min(128, kinds - start)
        out[pl.ds(start * count + place, width, stride=count), :] = stacked[
            :, start : start + width
        ].T


def relayout_rows(table, out, begin, rows):
    def step(place, carry):
        relayout(table, begin + place, out, place, rows)
        return carry

    lax.fori_loop(0, rows, step, 0, unroll=8)


def table_kernel(rows, count, table, out, count_out):
    count_out[0] = count[0]
    relayout_rows(table, out, 0, rows)


def halo_places(leaves):
    margin = leaves // 2
    even = lax.rem(lax.axis_index("dev"), 2) == 0
    return jnp.where(even, margin + leaves, 0), jnp.where(even, 0, margin + leaves)


def first_leaf(leaves):
    return (lax.axis_index("grp") * lax.axis_size("dev") + lax.axis_index("dev")) * leaves


def near_kernel(
    steps, begin, rows, targets, sources, count, charges, first, second, blocks, table, out, table_out,
    window, total,
):
    chunk = blocks.shape[0] // steps
    leaves, r, panels = charges.shape
    margin = leaves // 2
    live = count[0]
    leaf_start = first_leaf(leaves)
    first_at, second_at = halo_places(leaves)
    window[pl.ds(margin, leaves)] = charges[...]
    window[pl.ds(first_at, margin)] = first[:margin, :r]
    window[pl.ds(second_at, margin)] = second[:, :r]
    total[...] = jnp.zeros_like(total)

    def picked(slot):
        return window[sources[slot] - leaf_start + margin]

    def step(index, carry):
        base = index * chunk
        products = []
        for u in range(0, chunk, 2):
            both = lax.dot_general(
                jnp.concatenate([picked(base + u), picked(base + u + 1)], axis=0),
                blocks[pl.ds(base + u, 2)].reshape(2 * panels, panels),
                NT, preferred_element_type=F32,
            )
            products += [both[:r, :panels], both[r:, panels:]]
        for u in range(rows // steps):
            place = index * (rows // steps) + u
            relayout(table, begin + place, table_out, place, rows)
        for u in range(chunk):
            slot = base + u
            row = jnp.where(slot < live, targets[slot] - leaf_start, leaves)
            total[row] = total[row] + products[u]
        return carry

    lax.fori_loop(0, steps, step, 0)
    out[...] = total[:leaves]


def couple(tables, kind):
    return jnp.concatenate([table[kind] for table in tables], axis=0)


def far_kernel(
    parts, offsets, far, far_couple, dev_couple, grp_couple, moments, first, second, *rest
):
    tables = rest[:parts]
    out, box_tables, window, spread = rest[parts:]
    leaves, r, width = moments.shape
    margin = leaves // 2
    k, half = width // 2, width // 4
    nfar = far.shape[0]
    group = lax.axis_index("grp")
    origin = first_leaf(leaves) - margin
    first_at, second_at = halo_places(leaves)
    window[pl.ds(margin, leaves)] = moments[...]
    window[pl.ds(first_at, margin)] = first[:margin, r:]
    window[pl.ds(second_at, margin)] = second[:, r:]
    row = lax.broadcasted_iota(jnp.int32, (width, 4 * width), 0)
    column = lax.broadcasted_iota(jnp.int32, (width, 4 * width), 1)
    copier = (row == (column // width) * half + lax.rem(column, half)).astype(BF16)
    piece = 8
    for start in range(0, 2 * leaves, piece):
        rows = window[start : start + piece].reshape(piece * r, width)
        copied = jnp.dot(rows, copier, preferred_element_type=F32).astype(BF16)
        for section in range(4):
            spread[start : start + piece, section * r : (section + 1) * r] = copied[
                :, section * width : (section + 1) * width
            ].reshape(piece, r, width)
    lane = lax.broadcasted_iota(jnp.int32, (4 * r, width), 1) // half
    for leaf in range(leaves):
        lhs, rhs = [], []
        for quad in range(nfar // 4):
            picked = None
            taken = []
            for q in range(4):
                f = quad * 4 + q
                source = spread[far[f, leaf] - origin]
                picked = source if q == 0 else jnp.where(lane >= q, source, picked)
                taken.append(couple(tables, far_couple[f, leaf]))
            lhs.append(picked)
            rhs.append(jnp.concatenate(split(jnp.concatenate(taken, axis=0)), axis=1))
        product = jnp.dot(
            jnp.concatenate(lhs, axis=1), jnp.concatenate(rhs, axis=0),
            preferred_element_type=F32,
        )
        product = product[: 2 * r] + product[2 * r :]
        out[leaf] = fold(product[:, :width] + product[:, width:])
    wanted = [
        grp_couple[group, jnp.bitwise_xor(group, other)] for other in offsets[1:]
    ] + [dev_couple[0, n] for n in range(dev_couple.shape[1])]
    for i, kind in enumerate(wanted):
        box_tables[i * half : (i + 1) * half] = couple(tables, kind)


def final_kernel(
    steps, leaf_trans, dev_trans, dev_list, near, far, box_tables, boxes, groups, basis_t,
    trans_leaf, trans_dev, out_hbm, out, locals_, sems,
):
    leaves = near.shape[0]
    kinds, k, _ = trans_leaf.shape
    others = groups.shape[0] - 1
    group = lax.axis_index("grp")
    member = lax.axis_index("dev")
    split_at = others * (k // 2)
    lhs = [halves(groups[other + 1]) for other in range(others)]
    group_local = fold(dot3(jnp.concatenate(lhs, axis=1), box_tables[:split_at]))
    lhs = []
    for n in range(dev_list.shape[1]):
        place = jnp.bitwise_xor(dev_list[0, n] - group * lax.axis_size("dev"), member)
        lhs.append(halves(boxes[place]))
    listed = fold(dot3(jnp.concatenate(lhs, axis=1), box_tables[split_at:]))
    box_local = dot3(group_local, trans_dev[dev_trans[0]], NT) + listed
    by_kind = dot3(box_local, trans_leaf[...].reshape(kinds * k, k), NT)
    for kind in range(kinds):
        locals_[kind] = by_kind[:, kind * k : (kind + 1) * k]
    size = leaves // steps
    copies = []
    for i in range(steps):
        for leaf in range(i * size, (i + 1) * size):
            leaf_local = (locals_[leaf_trans[leaf]] + far[leaf]).astype(BF16)
            out[leaf] = near[leaf] + jnp.dot(
                leaf_local, basis_t[leaf], preferred_element_type=F32
            )
        piece = pl.ds(i * size, size)
        copies.append(pltpu.make_async_copy(out.at[piece], out_hbm.at[piece], sems.at[i]))
        copies[-1].start()
    for copy in copies:
        copy.wait()


def swap(x, axis, distance):
    return lax.ppermute(x, axis, [(i, i ^ distance) for i in range(lax.axis_size(axis))])


def cost(us):
    return pl.CostEstimate(flops=0, bytes_accessed=us * 3 * MIB, transcendentals=0)


def params(mib):
    return pltpu.CompilerParams(vmem_limit_bytes=mib * MIB)


def local(
    charges,
    leaf_basis,
    near_blocks,
    near_target,
    near_source,
    near_count,
    leaf_far,
    leaf_far_couple,
    leaf_trans,
    dev_trans,
    dev_list,
    dev_couple,
    grp_couple,
    trans_leaf,
    trans_dev,
    couple_table,
):
    leaves, r, panels = charges.shape
    k = leaf_basis.shape[2]
    margin = leaves // 2
    slots = near_blocks.shape[0]
    kinds = couple_table.shape[0]
    half = k // 2
    per_group = lax.axis_size("dev")
    devices = per_group * lax.axis_size("grp")
    basis_t = jnp.swapaxes(leaf_basis, 1, 2)
    shape = jax.ShapeDtypeStruct

    (
        moments, send_first, send_second, sums, leaf_kinds, dev_kind, own_charges, basis,
        leaf_maps, dev_maps, raw,
    ) = (
        pl.pallas_call(
            moment_kernel,
            out_shape=(
                shape((leaves, r, 2 * k), BF16),
                shape((margin, 2 * r, panels), BF16),
                shape((margin, 2 * r, panels), BF16),
                shape((r, 2 * k), F32),
                shape(leaf_trans.shape, jnp.int32),
                shape((8,), jnp.int32),
                shape(charges.shape, BF16),
                shape(basis_t.shape, BF16),
                shape(trans_leaf.shape, F32),
                shape(trans_dev.shape, F32),
                shape((2, half, k, kinds), F32),
            ),
            in_specs=[HBM, SMEM] + [HBM] * 5,
            out_specs=(VMEM,) * 4 + (SMEM,) * 2 + (VMEM,) * 5,
            scratch_shapes=[
                pltpu.VMEM((trans_leaf.shape[0], r, 2 * k), F32),
                pltpu.SemaphoreType.DMA((6,)),
            ],
            compiler_params=params(24),
            name="moments",
        )(
            pltpu.with_memory_space_constraint(leaf_trans, pltpu.HBM),
            dev_trans,
            pltpu.with_memory_space_constraint(charges, pltpu.HBM),
            pltpu.with_memory_space_constraint(basis_t, pltpu.HBM),
            pltpu.with_memory_space_constraint(trans_leaf, pltpu.HBM),
            pltpu.with_memory_space_constraint(trans_dev, pltpu.HBM),
            pltpu.with_memory_space_constraint(jnp.transpose(couple_table, (1, 2, 0)).reshape(2, half, k, kinds), pltpu.HBM),
        )
    )

    peer = swap(sums, "dev", 1)
    partners = [(i, i + 1) for i in range(1, devices - 1, 2)] + [(0, devices - 1)]
    second = lax.ppermute(send_second, AXES, partners + [(j, i) for i, j in partners])
    first = swap(send_first, "dev", 1)
    boxes = jnp.stack([sums[:, :k], peer[:, :k]])
    groups = (sums + peer)[None, :, k:]
    boxes, groups, raw = lax.optimization_barrier((boxes, groups, raw))

    offsets = [0]
    for distance in [2 << i for i in range((lax.axis_size("grp") // 2).bit_length() - 1)]:
        groups = jnp.concatenate([groups, swap(groups, "grp", distance)])
        offsets += [offset ^ distance for offset in offsets]
    high_rows = half // 4
    low_rows = half - high_rows
    table_low, live = pl.pallas_call(
        functools.partial(table_kernel, low_rows),
        out_shape=(shape((kinds * low_rows, 2 * k), F32), shape((8,), jnp.int32)),
        in_specs=[SMEM, VMEM],
        out_specs=(VMEM, SMEM),
        compiler_params=params(16),
        cost_estimate=cost(3),
        name="table",
    )(near_count, raw)
    groups, table_low, live, first, second = lax.optimization_barrier(
        (groups, table_low, live, first, second)
    )
    groups = jnp.concatenate([groups, swap(groups, "grp", 1)])
    offsets += [offset ^ 1 for offset in offsets]

    steps = 4

    def near_part():
        return pl.pallas_call(
            functools.partial(near_kernel, steps, low_rows, high_rows),
            out_shape=(
                shape((leaves, r, panels), F32),
                shape((kinds * high_rows, 2 * k), F32),
            ),
            in_specs=[SMEM, SMEM, SMEM, VMEM, VMEM, VMEM, VMEM, VMEM],
            out_specs=(VMEM, VMEM),
            scratch_shapes=[
                pltpu.VMEM((2 * leaves, r, panels), BF16),
                pltpu.VMEM((leaves + 1, r, panels), F32),
            ],
            compiler_params=params(16),
            cost_estimate=cost(3),
            name="near",
        )(
            near_target, near_source, live, own_charges, first, second,
            near_blocks, raw,
        )

    near, table_high = near_part()
    boxes, groups, near, table_high = lax.optimization_barrier((boxes, groups, near, table_high))
    parts = jnp.concatenate([boxes, groups])
    got = [swap(parts, "dev", distance) for distance in range(2, per_group, 2)]
    boxes = jnp.concatenate([boxes] + [part[:2] for part in got])
    groups = sum([part[2:] for part in got], start=groups)

    tables = [
        x.reshape(kinds, x.shape[0] // kinds, 2 * k) for x in (table_low, table_high)
    ]
    wanted = groups.shape[0] - 1 + dev_couple.shape[1]
    far, box_tables = pl.pallas_call(
        functools.partial(far_kernel, len(tables), tuple(offsets)),
        out_shape=(shape((leaves, r, k), F32), shape((wanted * half, 2 * k), F32)),
        in_specs=[SMEM] * 4 + [VMEM] * (3 + len(tables)),
        out_specs=(VMEM, VMEM),
        scratch_shapes=[
            pltpu.VMEM((2 * leaves, r, 2 * k), BF16),
            pltpu.VMEM((2 * leaves, 4 * r, 2 * k), BF16),
        ],
        compiler_params=params(16),
        cost_estimate=cost(3),
        name="far",
    )(
        leaf_far.T, leaf_far_couple.T, dev_couple, grp_couple, moments, first, second, *tables
    )

    return pl.pallas_call(
        functools.partial(final_kernel, steps),
        out_shape=shape((leaves, r, panels), F32),
        in_specs=[SMEM] * 3 + [VMEM] * 8,
        out_specs=HBM,
        scratch_shapes=[
            pltpu.VMEM((leaves, r, panels), F32),
            pltpu.VMEM((trans_leaf.shape[0], r, k), F32),
            pltpu.SemaphoreType.DMA((steps,)),
        ],
        compiler_params=params(16),
        name="final",
    )(
        leaf_kinds, dev_kind, dev_list, near, far, box_tables, boxes, groups, basis,
        leaf_maps, dev_maps,
    )


def solution(mesh):
    leaf = P(AXES)
    return jax.shard_map(
        local,
        mesh=mesh,
        in_specs=(leaf,) * 12 + (P(),) * 4,
        out_specs=leaf,
        check_vma=False,
    )
```

```python
import functools

import jax
import jax.numpy as jnp
from jax import lax
from jax.experimental import pallas as pl
from jax.experimental.pallas import tpu as pltpu
from jax.sharding import PartitionSpec as P

F32 = jnp.float32
BF16 = jnp.bfloat16
NT = (((1,), (1,)), ((), ()))
AXES = ("grp", "dev")
VMEM = pl.BlockSpec(memory_space=pltpu.VMEM)
SMEM = pl.BlockSpec(memory_space=pltpu.SMEM)
HBM = pl.BlockSpec(memory_space=pltpu.HBM)
MIB = 2**20
TABLE_ROWS = 4
PIECES = 4


def halves(x):
    half = x.shape[1] // 2
    return jnp.concatenate([x[:, :half], x[:, half:]], axis=0)


def fold(product):
    r, j = product.shape[0] // 2, product.shape[1] // 2
    return product[:r, :j] + product[r:, j:]


def split(x):
    high = x.astype(BF16)
    return high, (x - high.astype(F32)).astype(BF16)


def dot3(a, b, dims=(((1,), (0,)), ((), ()))):
    (a_high, a_low), (b_high, b_low) = split(a), split(b)
    both = lax.dot_general(
        jnp.concatenate([a_high, a_low], axis=0), b_high, dims, preferred_element_type=F32
    )
    rest = lax.dot_general(a_high, b_low, dims, preferred_element_type=F32)
    return both[: a.shape[0]] + both[a.shape[0] :] + rest


def moment_kernel(
    leaf_trans_hbm, dev_trans, charges_hbm, basis_hbm, trans_leaf_hbm, trans_dev_hbm, table_hbm,
    moments, send_first, send_second, sums, leaf_trans, dev_trans_out, charges, basis_t,
    trans_leaf, trans_dev, table, classes, sems,
):
    leaves, r, _ = charges.shape
    k = basis_t.shape[1]
    margin = leaves // 2
    kinds = trans_leaf.shape[0]
    size = leaves // PIECES
    pieces = [pl.ds(i * size, size) for i in range(PIECES)]
    moves = [(leaf_trans_hbm, leaf_trans), (charges_hbm, charges)]
    moves += [(basis_hbm.at[piece], basis_t.at[piece]) for piece in pieces]
    moves += [(trans_leaf_hbm, trans_leaf), (trans_dev_hbm, trans_dev)]
    moves += [
        (table_hbm.at[:, pl.ds(i, TABLE_ROWS)], table.at[:, pl.ds(i, TABLE_ROWS)])
        for i in range(0, table.shape[1], TABLE_ROWS)
    ]
    copies = [
        pltpu.make_async_copy(source, target, sems.at[i])
        for i, (source, target) in enumerate(moves)
    ]
    for copy in copies:
        copy.start()
    even = lax.rem(lax.axis_index("dev"), 2) == 0
    left = lax.broadcasted_iota(jnp.int32, (r, 2 * k), 1) < k
    for lane in range(PIECES):
        classes[lane][...] = jnp.zeros_like(classes[lane])
    copies[0].wait()
    copies[1].wait()
    for piece in range(PIECES):
        copies[2 + piece].wait()
        for leaf in range(piece * size, (piece + 1) * size):
            basis = basis_t[leaf]
            twice = lax.dot_general(
                charges[leaf], jnp.concatenate([basis, basis], axis=0), NT,
                preferred_element_type=F32,
            )
            kind = leaf_trans[leaf]
            lane = classes[leaf % PIECES]
            lane[kind] = lane[kind] + twice
            high = twice.astype(BF16).astype(F32)
            moments[leaf] = jnp.where(left, high, twice - high).astype(BF16)
    copies[2 + PIECES].wait()
    copies[3 + PIECES].wait()
    classes = sum([lane[...] for lane in classes[1:]], start=classes[0][...])
    lhs = [
        jnp.where(left, classes[kind], classes[kind + 1]) for kind in range(0, kinds, 2)
    ]
    box = dot3(jnp.concatenate(lhs, axis=1), trans_leaf[...].reshape(kinds * k, k))
    dev_trans_out[0] = dev_trans[0]
    up = dot3(box, trans_dev[dev_trans[0]])
    both = jnp.concatenate([box, up], axis=1)
    sums[...] = both

    def fill(first_from, second_from):
        for leaf in range(margin):
            send_first[leaf, :r] = charges[first_from + leaf]
            send_first[leaf, r:] = moments[first_from + leaf]
            send_second[leaf, :r] = charges[second_from + leaf]
            send_second[leaf, r:] = moments[second_from + leaf]

    @pl.when(even)
    def _():
        fill(margin, 0)

    @pl.when(jnp.logical_not(even))
    def _():
        fill(0, margin)

    for copy in copies[4 + PIECES :]:
        copy.wait()


def relayout(table, row, out, place, count):
    kinds = table.shape[3]
    stacked = jnp.concatenate([table[0, row], table[1, row]], axis=0)
    for start in range(0, kinds, 128):
        width = min(128, kinds - start)
        out[pl.ds(start * count + place, width, stride=count), :] = stacked[
            :, start : start + width
        ].T


def relayout_rows(table, out, begin, count, rows):
    def step(row, carry):
        relayout(table, row, out, begin + row, rows)
        return carry

    lax.fori_loop(0, count, step, 0, unroll=8)


def table_kernel(table, high_hbm, out, high, sems):
    low_rows, high_rows = table.shape[1], high.shape[1]
    copies = [
        pltpu.make_async_copy(
            high_hbm.at[:, pl.ds(low_rows + i, TABLE_ROWS)],
            high.at[:, pl.ds(i, TABLE_ROWS)],
            sems.at[i // TABLE_ROWS],
        )
        for i in range(0, high_rows, TABLE_ROWS)
    ]
    for copy in copies:
        copy.start()
    rows = out.shape[0] // table.shape[3]
    relayout_rows(table, out, 0, low_rows, rows)
    for copy in copies:
        copy.wait()
    relayout_rows(high, out, low_rows, rows - low_rows, rows)


def halo_places(leaves):
    margin = leaves // 2
    even = lax.rem(lax.axis_index("dev"), 2) == 0
    return jnp.where(even, margin + leaves, 0), jnp.where(even, 0, margin + leaves)


def first_leaf(leaves):
    return (lax.axis_index("grp") * lax.axis_size("dev") + lax.axis_index("dev")) * leaves


def near_kernel(
    steps, begin, rows, targets, sources, count, charges, first, second, blocks, table, out, table_out,
    window, total,
):
    chunk = blocks.shape[0] // steps
    leaves, r, panels = charges.shape
    margin = leaves // 2
    live = count[...]
    leaf_start = first_leaf(leaves)
    first_at, second_at = halo_places(leaves)
    window[pl.ds(margin, leaves)] = charges[...]
    window[pl.ds(first_at, margin)] = first[:margin, :r]
    window[pl.ds(second_at, margin)] = second[:, :r]
    total[...] = jnp.zeros_like(total)

    def picked(slot):
        return window[sources[slot] - leaf_start + margin]

    def step(index, carry):
        base = index * chunk
        products = []
        empty = jnp.zeros((r, panels), BF16)
        for u in [base + i for i in range(0, chunk, 4)]:
            one, two, three, four = (picked(u + i) for i in range(4))
            lhs = jnp.concatenate([one, empty, three, empty], axis=0)
            rhs = jnp.concatenate([empty, two, empty, four], axis=0)
            both = lax.dot_general(
                jnp.concatenate([lhs, rhs], axis=1),
                jnp.concatenate(
                    [
                        jnp.concatenate([blocks[u], blocks[u + 2]], axis=0),
                        jnp.concatenate([blocks[u + 1], blocks[u + 3]], axis=0),
                    ],
                    axis=1,
                ),
                NT, preferred_element_type=F32,
            )
            products += [both[:r, :panels], both[r : 2 * r, :panels]]
            products += [both[2 * r : 3 * r, panels:], both[3 * r :, panels:]]
        for u in range(rows // steps):
            place = index * (rows // steps) + u
            relayout(table, begin + place, table_out, place, rows)
        for u in range(chunk):
            slot = base + u
            row = targets[slot] - leaf_start
            total[row] = total[row] + jnp.where(live > slot, products[u], 0.0)
        return carry

    lax.fori_loop(0, steps, step, 0)
    out[...] = total[...]


def couple(tables, kind):
    return jnp.concatenate([table[kind] for table in tables], axis=0)


def spread_kernel(count, moments, first, second, spread, count_out, window):
    count_out[...] = jnp.full(count_out.shape, count[0], jnp.int32)
    leaves, r, width = moments.shape
    margin = leaves // 2
    half = width // 4
    first_at, second_at = halo_places(leaves)
    window[pl.ds(margin, leaves)] = moments[...]
    window[pl.ds(first_at, margin)] = first[:margin, r:]
    window[pl.ds(second_at, margin)] = second[:, r:]
    row = lax.broadcasted_iota(jnp.int32, (width, 4 * width), 0)
    column = lax.broadcasted_iota(jnp.int32, (width, 4 * width), 1)
    copier = (row == (column // width) * half + lax.rem(column, half)).astype(BF16)
    piece = 8
    for start in range(0, 2 * leaves, piece):
        rows = window[start : start + piece].reshape(piece * r, width)
        copied = jnp.dot(rows, copier, preferred_element_type=F32).astype(BF16)
        for section in range(4):
            spread[start : start + piece, section * r : (section + 1) * r] = copied[
                :, section * width : (section + 1) * width
            ].reshape(piece, r, width)


def far_kernel(parts, offsets, far, far_couple, dev_couple, grp_couple, spread, *rest):
    tables = rest[:parts]
    out, box_tables = rest[parts:]
    leaves, r, k = out.shape
    width, half = 2 * k, k // 2
    nfar = far.shape[0]
    group = lax.axis_index("grp")
    origin = first_leaf(leaves) - leaves // 2
    lane = lax.broadcasted_iota(jnp.int32, (4 * r, width), 1) // half
    for leaf in range(leaves):
        lhs, rhs = [], []
        for quad in range(nfar // 4):
            picked = None
            taken = []
            for q in range(4):
                f = quad * 4 + q
                source = spread[far[f, leaf] - origin]
                picked = source if q == 0 else jnp.where(lane >= q, source, picked)
                taken.append(couple(tables, far_couple[f, leaf]))
            lhs.append(picked)
            rhs.append(jnp.concatenate(split(jnp.concatenate(taken, axis=0)), axis=1))
        product = jnp.dot(
            jnp.concatenate(lhs, axis=1), jnp.concatenate(rhs, axis=0),
            preferred_element_type=F32,
        )
        product = product[: 2 * r] + product[2 * r :]
        out[leaf] = fold(product[:, :width] + product[:, width:])
    wanted = [
        grp_couple[group, jnp.bitwise_xor(group, other)] for other in offsets[1:]
    ] + [dev_couple[0, n] for n in range(dev_couple.shape[1])]
    for i, kind in enumerate(wanted):
        box_tables[i * half : (i + 1) * half] = couple(tables, kind)


def final_kernel(
    steps, leaf_trans, dev_trans, dev_list, near, far, box_tables, boxes, groups, basis_t,
    trans_leaf, trans_dev, out_hbm, out, locals_, sems,
):
    leaves = near.shape[0]
    kinds, k, _ = trans_leaf.shape
    others = groups.shape[0] - 1
    group = lax.axis_index("grp")
    member = lax.axis_index("dev")
    split_at = others * (k // 2)
    lhs = [halves(groups[other + 1]) for other in range(others)]
    group_local = fold(dot3(jnp.concatenate(lhs, axis=1), box_tables[:split_at]))
    lhs = []
    for n in range(dev_list.shape[1]):
        place = jnp.bitwise_xor(dev_list[0, n] - group * lax.axis_size("dev"), member)
        lhs.append(halves(boxes[place]))
    listed = fold(dot3(jnp.concatenate(lhs, axis=1), box_tables[split_at:]))
    box_local = dot3(group_local, trans_dev[dev_trans[0]], NT) + listed
    by_kind = dot3(box_local, trans_leaf[...].reshape(kinds * k, k), NT)
    for kind in range(kinds):
        locals_[kind] = by_kind[:, kind * k : (kind + 1) * k]
    size = leaves // steps
    copies = []
    for i in range(steps):
        for leaf in range(i * size, (i + 1) * size):
            leaf_local = (locals_[leaf_trans[leaf]] + far[leaf]).astype(BF16)
            out[leaf] = near[leaf] + jnp.dot(
                leaf_local, basis_t[leaf], preferred_element_type=F32
            )
        piece = pl.ds(i * size, size)
        copies.append(pltpu.make_async_copy(out.at[piece], out_hbm.at[piece], sems.at[i]))
        copies[-1].start()
    for copy in copies:
        copy.wait()


def swap(x, axis, distance):
    return lax.ppermute(x, axis, [(i, i ^ distance) for i in range(lax.axis_size(axis))])


def side_by_side(first, second, move):
    parts = jnp.concatenate([first, second])
    total, _, k = parts.shape
    half = (total + 1) // 2
    parts = jnp.pad(parts, ((0, 2 * half - total), (0, 0), (0, 0)))
    got = move(jnp.concatenate([parts[:half], parts[half:]], axis=2))
    return jnp.concatenate([got[:, :, :k], got[:, :, k:]])[:total]


def cost(us):
    return pl.CostEstimate(flops=0, bytes_accessed=us * 3 * MIB, transcendentals=0)


def params(mib):
    return pltpu.CompilerParams(vmem_limit_bytes=mib * MIB)


def local(
    charges,
    leaf_basis,
    near_blocks,
    near_target,
    near_source,
    near_count,
    leaf_far,
    leaf_far_couple,
    leaf_trans,
    dev_trans,
    dev_list,
    dev_couple,
    grp_couple,
    trans_leaf,
    trans_dev,
    couple_table,
):
    leaves, r, panels = charges.shape
    k = leaf_basis.shape[2]
    margin = leaves // 2
    slots = near_blocks.shape[0]
    kinds = couple_table.shape[0]
    half = k // 2
    per_group = lax.axis_size("dev")
    devices = per_group * lax.axis_size("grp")
    basis_t = jnp.swapaxes(leaf_basis, 1, 2)
    shape = jax.ShapeDtypeStruct

    couplings = pltpu.with_memory_space_constraint(
        jnp.transpose(couple_table, (1, 2, 0)).reshape(2, half, k, kinds), pltpu.HBM
    )
    (
        moments, send_first, send_second, sums, leaf_kinds, dev_kind, own_charges, basis,
        leaf_maps, dev_maps, raw,
    ) = (
        pl.pallas_call(
            moment_kernel,
            out_shape=(
                shape((leaves, r, 2 * k), BF16),
                shape((margin, 2 * r, panels), BF16),
                shape((margin, 2 * r, panels), BF16),
                shape((r, 2 * k), F32),
                shape(leaf_trans.shape, jnp.int32),
                shape((8,), jnp.int32),
                shape(charges.shape, BF16),
                shape(basis_t.shape, BF16),
                shape(trans_leaf.shape, F32),
                shape(trans_dev.shape, F32),
                shape((2, half // 2, k, kinds), F32),
            ),
            in_specs=[HBM, SMEM] + [HBM] * 5,
            out_specs=(VMEM,) * 4 + (SMEM,) * 2 + (VMEM,) * 5,
            scratch_shapes=[
                [pltpu.VMEM((trans_leaf.shape[0], r, 2 * k), F32) for _ in range(PIECES)],
                pltpu.SemaphoreType.DMA((4 + PIECES + half // 2 // TABLE_ROWS,)),
            ],
            compiler_params=params(24),
            name="moments",
        )(
            pltpu.with_memory_space_constraint(leaf_trans, pltpu.HBM),
            dev_trans,
            pltpu.with_memory_space_constraint(charges, pltpu.HBM),
            pltpu.with_memory_space_constraint(basis_t, pltpu.HBM),
            pltpu.with_memory_space_constraint(trans_leaf, pltpu.HBM),
            pltpu.with_memory_space_constraint(trans_dev, pltpu.HBM),
            couplings,
        )
    )

    first = swap(send_first, "dev", 1)
    peer = swap(sums, "dev", 1)
    partners = [(i, i + 1) for i in range(1, devices - 1, 2)] + [(0, devices - 1)]
    second = lax.ppermute(send_second, AXES, partners + [(j, i) for i, j in partners])
    boxes = jnp.stack([sums[:, :k], peer[:, :k]])
    groups = (sums + peer)[None, :, k:]
    boxes, groups, raw = lax.optimization_barrier((boxes, groups, raw))
    offsets = [0]
    for distance in [2 << i for i in range((lax.axis_size("grp") // 2).bit_length() - 1)]:
        groups = jnp.concatenate([groups, swap(groups, "grp", distance)])
        offsets += [offset ^ distance for offset in offsets]
    high_rows = half // 4
    low_rows = half - high_rows
    table_low, raw = pl.pallas_call(
        table_kernel,
        out_shape=(
            shape((kinds * low_rows, 2 * k), F32),
            shape((2, half // 2, k, kinds), F32),
        ),
        in_specs=[VMEM, HBM],
        out_specs=(VMEM, VMEM),
        scratch_shapes=[pltpu.SemaphoreType.DMA((half // 2 // TABLE_ROWS,))],
        compiler_params=params(16),
        cost_estimate=cost(3),
        name="table",
    )(raw, couplings)
    groups, table_low, first, second = lax.optimization_barrier(
        (groups, table_low, first, second)
    )
    groups = jnp.concatenate([groups, swap(groups, "grp", 1)])
    offsets += [offset ^ 1 for offset in offsets]
    spread, live = pl.pallas_call(
        spread_kernel,
        out_shape=(shape((2 * leaves, 4 * r, 2 * k), BF16), shape((r, panels), jnp.int32)),
        in_specs=[SMEM] + [VMEM] * 3,
        out_specs=(VMEM, VMEM),
        scratch_shapes=[pltpu.VMEM((2 * leaves, r, 2 * k), BF16)],
        compiler_params=params(16),
        cost_estimate=cost(1),
        name="spread",
    )(near_count, moments, first, second)
    groups, spread, live, first, second = lax.optimization_barrier(
        (groups, spread, live, first, second)
    )
    steps = 2

    def near_part():
        return pl.pallas_call(
            functools.partial(near_kernel, steps, low_rows - half // 2, high_rows),
            out_shape=(
                shape((leaves, r, panels), F32),
                shape((kinds * high_rows, 2 * k), F32),
            ),
            in_specs=[SMEM] * 2 + [VMEM] * 6,
            out_specs=(VMEM, VMEM),
            scratch_shapes=[
                pltpu.VMEM((2 * leaves, r, panels), BF16),
                pltpu.VMEM((leaves, r, panels), F32),
            ],
            compiler_params=params(16),
            cost_estimate=cost(3),
            name="near",
        )(
            near_target, near_source, live, own_charges, first, second,
            near_blocks, raw,
        )

    near = None
    for distance in [2 << i for i in range((per_group // 2).bit_length() - 1)]:
        count = boxes.shape[0]
        got = side_by_side(boxes, groups, functools.partial(swap, axis="dev", distance=distance))
        boxes = jnp.concatenate([boxes, got[:count]])
        groups = groups + got[count:]
        if near is None:
            near, table_high = near_part()
            boxes, groups, near, table_high = lax.optimization_barrier(
                (boxes, groups, near, table_high)
            )

    tables = [
        x.reshape(kinds, x.shape[0] // kinds, 2 * k) for x in (table_low, table_high)
    ]
    wanted = groups.shape[0] - 1 + dev_couple.shape[1]
    far, box_tables = pl.pallas_call(
        functools.partial(far_kernel, len(tables), tuple(offsets)),
        out_shape=(shape((leaves, r, k), F32), shape((wanted * half, 2 * k), F32)),
        in_specs=[SMEM] * 4 + [VMEM] * (1 + len(tables)),
        out_specs=(VMEM, VMEM),
        compiler_params=params(16),
        cost_estimate=cost(3),
        name="far",
    )(
        leaf_far.T, leaf_far_couple.T, dev_couple, grp_couple, spread, *tables
    )

    return pl.pallas_call(
        functools.partial(final_kernel, 8),
        out_shape=shape((leaves, r, panels), F32),
        in_specs=[SMEM] * 3 + [VMEM] * 8,
        out_specs=HBM,
        scratch_shapes=[
            pltpu.VMEM((leaves, r, panels), F32),
            pltpu.VMEM((trans_leaf.shape[0], r, k), F32),
            pltpu.SemaphoreType.DMA((8,)),
        ],
        compiler_params=params(16),
        name="final",
    )(
        leaf_kinds, dev_kind, dev_list, near, far, box_tables, boxes, groups, basis,
        leaf_maps, dev_maps,
    )


def solution(mesh):
    leaf = P(AXES)
    return jax.shard_map(
        local,
        mesh=mesh,
        in_specs=(leaf,) * 12 + (P(),) * 4,
        out_specs=leaf,
        check_vma=False,
    )
```

```python
import functools

import jax
import jax.numpy as jnp
from jax import lax
from jax.experimental import pallas as pl
from jax.experimental.pallas import tpu as pltpu
from jax.sharding import PartitionSpec as P

F32 = jnp.float32
BF16 = jnp.bfloat16
NT = (((1,), (1,)), ((), ()))
AXES = ("grp", "dev")
VMEM = pl.BlockSpec(memory_space=pltpu.VMEM)
SMEM = pl.BlockSpec(memory_space=pltpu.SMEM)
HBM = pl.BlockSpec(memory_space=pltpu.HBM)
MIB = 2**20
TABLE_ROWS = 8
PIECES = 4


def halves(x):
    half = x.shape[1] // 2
    return jnp.concatenate([x[:, :half], x[:, half:]], axis=0)


def fold(product):
    r, j = product.shape[0] // 2, product.shape[1] // 2
    return product[:r, :j] + product[r:, j:]


def split(x):
    high = x.astype(BF16)
    return high, (x - high.astype(F32)).astype(BF16)


def dot3(a, b, dims=(((1,), (0,)), ((), ()))):
    (a_high, a_low), (b_high, b_low) = split(a), split(b)
    both = lax.dot_general(
        jnp.concatenate([a_high, a_low], axis=0), b_high, dims, preferred_element_type=F32
    )
    rest = lax.dot_general(a_high, b_low, dims, preferred_element_type=F32)
    return both[: a.shape[0]] + both[a.shape[0] :] + rest


def moment_kernel(
    leaf_trans_hbm, dev_trans, charges_hbm, basis_hbm, trans_leaf_hbm, trans_dev_hbm, table_hbm,
    moments, send_first, send_second, sums, leaf_trans, dev_trans_out, charges, basis_t,
    trans_leaf, trans_dev, table, classes, sems,
):
    leaves, r, _ = charges.shape
    k = basis_t.shape[1]
    margin = leaves // 2
    kinds = trans_leaf.shape[0]
    size = leaves // PIECES
    moves = [(basis_hbm, basis_t), (charges_hbm, charges), (leaf_trans_hbm, leaf_trans)]
    moves += [(trans_leaf_hbm, trans_leaf), (trans_dev_hbm, trans_dev)]
    moves += [
        (table_hbm.at[:, pl.ds(i, TABLE_ROWS)], table.at[:, pl.ds(i, TABLE_ROWS)])
        for i in range(0, table.shape[1], TABLE_ROWS)
    ]
    copies = [
        pltpu.make_async_copy(source, target, sems.at[i])
        for i, (source, target) in enumerate(moves)
    ]
    for copy in copies:
        copy.start()
    even = lax.rem(lax.axis_index("dev"), 2) == 0
    left = lax.broadcasted_iota(jnp.int32, (r, 2 * k), 1) < k
    for lane in range(PIECES):
        classes[lane][...] = jnp.zeros_like(classes[lane])
    for copy in copies[:3]:
        copy.wait()
    for piece in range(PIECES):
        for leaf in range(piece * size, (piece + 1) * size):
            basis = basis_t[leaf]
            twice = lax.dot_general(
                charges[leaf], jnp.concatenate([basis, basis], axis=0), NT,
                preferred_element_type=F32,
            )
            kind = leaf_trans[leaf]
            lane = classes[leaf % PIECES]
            lane[kind] = lane[kind] + twice
            high = twice.astype(BF16).astype(F32)
            moments[leaf] = jnp.where(left, high, twice - high).astype(BF16)
    copies[3].wait()
    copies[4].wait()
    classes = sum([lane[...] for lane in classes[1:]], start=classes[0][...])
    lhs = [
        jnp.where(left, classes[kind], classes[kind + 1]) for kind in range(0, kinds, 2)
    ]
    box = dot3(jnp.concatenate(lhs, axis=1), trans_leaf[...].reshape(kinds * k, k))
    dev_trans_out[0] = dev_trans[0]
    up = dot3(box, trans_dev[dev_trans[0]])
    both = jnp.concatenate([box, up], axis=1)
    sums[...] = both

    def fill(first_from, second_from):
        for leaf in range(margin):
            send_first[leaf, :r] = charges[first_from + leaf]
            send_first[leaf, r:] = moments[first_from + leaf]
            send_second[leaf, :r] = charges[second_from + leaf]
            send_second[leaf, r:] = moments[second_from + leaf]

    @pl.when(even)
    def _():
        fill(margin, 0)

    @pl.when(jnp.logical_not(even))
    def _():
        fill(0, margin)

    for copy in copies[5:]:
        copy.wait()


def relayout(table, row, out, place, count):
    kinds = table.shape[3]
    stacked = jnp.concatenate([table[0, row], table[1, row]], axis=0)
    for start in range(0, kinds, 128):
        width = min(128, kinds - start)
        out[pl.ds(start * count + place, width, stride=count), :] = stacked[
            :, start : start + width
        ].T


def relayout_rows(table, out, begin, count, rows):
    def step(row, carry):
        relayout(table, row, out, begin + row, rows)
        return carry

    lax.fori_loop(0, count, step, 0, unroll=8)


def table_kernel(table, high_hbm, out, high, sems):
    low_rows, high_rows = table.shape[1], high.shape[1]
    copies = [
        pltpu.make_async_copy(
            high_hbm.at[:, pl.ds(low_rows + i, TABLE_ROWS)],
            high.at[:, pl.ds(i, TABLE_ROWS)],
            sems.at[i // TABLE_ROWS],
        )
        for i in range(0, high_rows, TABLE_ROWS)
    ]
    for copy in copies:
        copy.start()
    rows = out.shape[0] // table.shape[3]
    relayout_rows(table, out, 0, low_rows, rows)
    for copy in copies:
        copy.wait()
    relayout_rows(high, out, low_rows, rows - low_rows, rows)


def halo_places(leaves):
    margin = leaves // 2
    even = lax.rem(lax.axis_index("dev"), 2) == 0
    return jnp.where(even, margin + leaves, 0), jnp.where(even, 0, margin + leaves)


def first_leaf(leaves):
    return (lax.axis_index("grp") * lax.axis_size("dev") + lax.axis_index("dev")) * leaves


def near_kernel(
    steps, begin, rows, targets, sources, count, charges, first, second, blocks, table, out, table_out,
    window, total,
):
    chunk = blocks.shape[0] // steps
    leaves, r, panels = charges.shape
    margin = leaves // 2
    live = count[...]
    leaf_start = first_leaf(leaves)
    first_at, second_at = halo_places(leaves)
    window[pl.ds(margin, leaves)] = charges[...]
    window[pl.ds(first_at, margin)] = first[:margin, :r]
    window[pl.ds(second_at, margin)] = second[:, :r]
    total[...] = jnp.zeros_like(total)

    def picked(slot):
        return window[sources[slot] - leaf_start + margin]

    def step(index, carry):
        base = index * chunk
        products = []
        empty = jnp.zeros((r, panels), BF16)
        for u in [base + i for i in range(0, chunk, 4)]:
            one, two, three, four = (picked(u + i) for i in range(4))
            lhs = jnp.concatenate([one, empty, three, empty], axis=0)
            rhs = jnp.concatenate([empty, two, empty, four], axis=0)
            both = lax.dot_general(
                jnp.concatenate([lhs, rhs], axis=1),
                jnp.concatenate(
                    [
                        jnp.concatenate([blocks[u], blocks[u + 2]], axis=0),
                        jnp.concatenate([blocks[u + 1], blocks[u + 3]], axis=0),
                    ],
                    axis=1,
                ),
                NT, preferred_element_type=F32,
            )
            products += [both[:r, :panels], both[r : 2 * r, :panels]]
            products += [both[2 * r : 3 * r, panels:], both[3 * r :, panels:]]
        for u in range(rows // steps):
            place = index * (rows // steps) + u
            relayout(table, begin + place, table_out, place, rows)
        for u in range(chunk):
            slot = base + u
            row = targets[slot] - leaf_start
            total[row] = total[row] + jnp.where(live > slot, products[u], 0.0)
        return carry

    lax.fori_loop(0, steps, step, 0)
    out[...] = total[...]


def couple(tables, kind):
    return jnp.concatenate([table[kind] for table in tables], axis=0)


def spread_kernel(count, moments, first, second, spread, count_out, window):
    count_out[...] = jnp.full(count_out.shape, count[0], jnp.int32)
    leaves, r, width = moments.shape
    margin = leaves // 2
    half = width // 4
    first_at, second_at = halo_places(leaves)
    window[pl.ds(margin, leaves)] = moments[...]
    window[pl.ds(first_at, margin)] = first[:margin, r:]
    window[pl.ds(second_at, margin)] = second[:, r:]
    row = lax.broadcasted_iota(jnp.int32, (width, 4 * width), 0)
    column = lax.broadcasted_iota(jnp.int32, (width, 4 * width), 1)
    copier = (row == (column // width) * half + lax.rem(column, half)).astype(BF16)
    piece = 8
    for start in range(0, 2 * leaves, piece):
        rows = window[start : start + piece].reshape(piece * r, width)
        copied = jnp.dot(rows, copier, preferred_element_type=F32).astype(BF16)
        for section in range(4):
            spread[start : start + piece, section * r : (section + 1) * r] = copied[
                :, section * width : (section + 1) * width
            ].reshape(piece, r, width)


def far_kernel(
    parts, offsets, far, far_couple, dev_couple, grp_couple, spread, trans_leaf, *rest
):
    tables = rest[:parts]
    out, box_tables, leaf_maps = rest[parts:]
    pairs, r, width = out.shape
    leaves, k, half = 2 * pairs, width // 2, width // 4
    nfar = far.shape[0]
    group = lax.axis_index("grp")
    origin = first_leaf(leaves) - leaves // 2
    lane = lax.broadcasted_iota(jnp.int32, (4 * r, width), 1) // half
    for leaf in range(leaves):
        lhs, rhs = [], []
        for quad in range(nfar // 4):
            picked = None
            taken = []
            for q in range(4):
                f = quad * 4 + q
                source = spread[far[f, leaf] - origin]
                picked = source if q == 0 else jnp.where(lane >= q, source, picked)
                taken.append(couple(tables, far_couple[f, leaf]))
            lhs.append(picked)
            rhs.append(jnp.concatenate(split(jnp.concatenate(taken, axis=0)), axis=1))
        product = jnp.dot(
            jnp.concatenate(lhs, axis=1), jnp.concatenate(rhs, axis=0),
            preferred_element_type=F32,
        )
        product = product[: 2 * r] + product[2 * r :]
        product = product[:, :width] + product[:, width:]
        own, other = (product[:r], product[r:]) if leaf % 2 == 0 else (product[r:], product[:r])
        folded = own + pltpu.roll(other, k, 1)
        if leaf % 2 == 0:
            even_leaf = folded
        else:
            out[leaf // 2] = jnp.where(lane[:r] < 2, even_leaf, folded)
    for kind in range(0, trans_leaf.shape[0], 2):
        two = trans_leaf[kind : kind + 2].reshape(width, k).T
        high, low = split(two)
        leaf_maps[0, :, kind * k : (kind + 2) * k] = high
        leaf_maps[1, :, kind * k : (kind + 2) * k] = low
    wanted = [
        grp_couple[group, jnp.bitwise_xor(group, other)] for other in offsets[1:]
    ] + [dev_couple[0, n] for n in range(dev_couple.shape[1])]
    for i, kind in enumerate(wanted):
        box_tables[i * half : (i + 1) * half] = couple(tables, kind)


def final_kernel(
    steps, leaf_trans, dev_trans, dev_list, near, far, box_tables, boxes, groups, basis_t,
    leaf_maps, trans_dev, out_hbm, out, locals_, sems,
):
    leaves, r, panels = near.shape
    k = leaf_maps.shape[1]
    kinds = leaf_maps.shape[2] // k
    others = groups.shape[0] - 1
    group = lax.axis_index("grp")
    member = lax.axis_index("dev")
    split_at = others * (k // 2)
    lhs = [halves(groups[other + 1]) for other in range(others)]
    group_local = fold(dot3(jnp.concatenate(lhs, axis=1), box_tables[:split_at]))
    lhs = []
    for n in range(dev_list.shape[1]):
        place = jnp.bitwise_xor(dev_list[0, n] - group * lax.axis_size("dev"), member)
        lhs.append(halves(boxes[place]))
    listed = fold(dot3(jnp.concatenate(lhs, axis=1), box_tables[split_at:]))
    box_local = dot3(group_local, trans_dev[dev_trans[0]], NT) + listed
    high, low = split(box_local)
    by_kind = jnp.dot(
        jnp.concatenate([high, low], axis=0), leaf_maps[0], preferred_element_type=F32
    )
    by_kind = by_kind[:r] + by_kind[r:]
    by_kind += jnp.dot(high, leaf_maps[1], preferred_element_type=F32)
    left = lax.broadcasted_iota(jnp.int32, (r, 2 * k), 1) < k
    for kind in range(0, kinds, 2):
        two = by_kind[:, kind * k : (kind + 2) * k]
        turned = pltpu.roll(two, k, 1)
        locals_[kind] = jnp.where(left, two, turned)
        locals_[kind + 1] = jnp.where(left, turned, two)
    size = leaves // steps
    copies = []
    for i in range(steps):
        for leaf in range(i * size, (i + 1) * size, 4):
            lhs = []
            for u in range(4):
                whole = locals_[leaf_trans[leaf + u]] + far[(leaf + u) // 2]
                lhs.append(jnp.where(left if u % 2 == 0 else jnp.logical_not(left), whole, 0.0))
            rhs = [
                basis_t[leaf + u : leaf + u + 2].reshape(2 * k, panels) for u in range(0, 4, 2)
            ]
            product = jnp.dot(
                jnp.concatenate(lhs, axis=0).astype(BF16), jnp.concatenate(rhs, axis=1),
                preferred_element_type=F32,
            )
            for u in range(4):
                columns = slice(u // 2 * panels, (u // 2 + 1) * panels)
                out[leaf + u] = near[leaf + u] + product[u * r : (u + 1) * r, columns]
        piece = pl.ds(i * size, size)
        copies.append(pltpu.make_async_copy(out.at[piece], out_hbm.at[piece], sems.at[i]))
        copies[-1].start()
    for copy in copies:
        copy.wait()


def swap(x, axis, distance):
    return lax.ppermute(x, axis, [(i, i ^ distance) for i in range(lax.axis_size(axis))])


def side_by_side(first, second, move):
    parts = jnp.concatenate([first, second])
    total, _, k = parts.shape
    half = (total + 1) // 2
    parts = jnp.pad(parts, ((0, 2 * half - total), (0, 0), (0, 0)))
    got = move(jnp.concatenate([parts[:half], parts[half:]], axis=2))
    return jnp.concatenate([got[:, :, :k], got[:, :, k:]])[:total]


def cost(us):
    return pl.CostEstimate(flops=0, bytes_accessed=us * 3 * MIB, transcendentals=0)


def params(mib):
    return pltpu.CompilerParams(vmem_limit_bytes=mib * MIB)


def local(
    charges,
    leaf_basis,
    near_blocks,
    near_target,
    near_source,
    near_count,
    leaf_far,
    leaf_far_couple,
    leaf_trans,
    dev_trans,
    dev_list,
    dev_couple,
    grp_couple,
    trans_leaf,
    trans_dev,
    couple_table,
):
    leaves, r, panels = charges.shape
    k = leaf_basis.shape[2]
    margin = leaves // 2
    slots = near_blocks.shape[0]
    kinds = couple_table.shape[0]
    half = k // 2
    per_group = lax.axis_size("dev")
    devices = per_group * lax.axis_size("grp")
    basis_t = jnp.swapaxes(leaf_basis, 1, 2)
    shape = jax.ShapeDtypeStruct

    couplings = pltpu.with_memory_space_constraint(
        jnp.transpose(couple_table, (1, 2, 0)).reshape(2, half, k, kinds), pltpu.HBM
    )
    (
        moments, send_first, send_second, sums, leaf_kinds, dev_kind, own_charges, basis,
        leaf_maps, dev_maps, raw,
    ) = (
        pl.pallas_call(
            moment_kernel,
            out_shape=(
                shape((leaves, r, 2 * k), BF16),
                shape((margin, 2 * r, panels), BF16),
                shape((margin, 2 * r, panels), BF16),
                shape((r, 2 * k), F32),
                shape(leaf_trans.shape, jnp.int32),
                shape((8,), jnp.int32),
                shape(charges.shape, BF16),
                shape(basis_t.shape, BF16),
                shape(trans_leaf.shape, F32),
                shape(trans_dev.shape, F32),
                shape((2, half // 2, k, kinds), F32),
            ),
            in_specs=[HBM, SMEM] + [HBM] * 5,
            out_specs=(VMEM,) * 4 + (SMEM,) * 2 + (VMEM,) * 5,
            scratch_shapes=[
                [pltpu.VMEM((trans_leaf.shape[0], r, 2 * k), F32) for _ in range(PIECES)],
                pltpu.SemaphoreType.DMA((5 + half // 2 // TABLE_ROWS,)),
            ],
            compiler_params=params(24),
            name="moments",
        )(
            pltpu.with_memory_space_constraint(leaf_trans, pltpu.HBM),
            dev_trans,
            pltpu.with_memory_space_constraint(charges, pltpu.HBM),
            pltpu.with_memory_space_constraint(basis_t, pltpu.HBM),
            pltpu.with_memory_space_constraint(trans_leaf, pltpu.HBM),
            pltpu.with_memory_space_constraint(trans_dev, pltpu.HBM),
            couplings,
        )
    )

    first = swap(send_first, "dev", 1)
    peer = swap(sums, "dev", 1)
    partners = [(i, i + 1) for i in range(1, devices - 1, 2)] + [(0, devices - 1)]
    second = lax.ppermute(send_second, AXES, partners + [(j, i) for i, j in partners])
    boxes = jnp.stack([sums[:, :k], peer[:, :k]])
    groups = (sums + peer)[None, :, k:]
    boxes, groups, raw = lax.optimization_barrier((boxes, groups, raw))
    offsets = [0]
    for distance in [2 << i for i in range((lax.axis_size("grp") // 2).bit_length() - 1)]:
        groups = jnp.concatenate([groups, swap(groups, "grp", distance)])
        offsets += [offset ^ distance for offset in offsets]
    high_rows = half // 4
    low_rows = half - high_rows
    table_low, raw = pl.pallas_call(
        table_kernel,
        out_shape=(
            shape((kinds * low_rows, 2 * k), F32),
            shape((2, half // 2, k, kinds), F32),
        ),
        in_specs=[VMEM, HBM],
        out_specs=(VMEM, VMEM),
        scratch_shapes=[pltpu.SemaphoreType.DMA((half // 2 // TABLE_ROWS,))],
        compiler_params=params(16),
        cost_estimate=cost(3),
        name="table",
    )(raw, couplings)
    groups, table_low, first, second = lax.optimization_barrier(
        (groups, table_low, first, second)
    )
    groups = jnp.concatenate([groups, swap(groups, "grp", 1)])
    offsets += [offset ^ 1 for offset in offsets]
    spread, live = pl.pallas_call(
        spread_kernel,
        out_shape=(shape((2 * leaves, 4 * r, 2 * k), BF16), shape((r, panels), jnp.int32)),
        in_specs=[SMEM] + [VMEM] * 3,
        out_specs=(VMEM, VMEM),
        scratch_shapes=[pltpu.VMEM((2 * leaves, r, 2 * k), BF16)],
        compiler_params=params(16),
        cost_estimate=cost(1),
        name="spread",
    )(near_count, moments, first, second)
    groups, spread, live, first, second = lax.optimization_barrier(
        (groups, spread, live, first, second)
    )
    steps = 2

    def near_part():
        return pl.pallas_call(
            functools.partial(near_kernel, steps, low_rows - half // 2, high_rows),
            out_shape=(
                shape((leaves, r, panels), F32),
                shape((kinds * high_rows, 2 * k), F32),
            ),
            in_specs=[SMEM] * 2 + [VMEM] * 6,
            out_specs=(VMEM, VMEM),
            scratch_shapes=[
                pltpu.VMEM((2 * leaves, r, panels), BF16),
                pltpu.VMEM((leaves, r, panels), F32),
            ],
            compiler_params=params(16),
            cost_estimate=cost(3),
            name="near",
        )(
            near_target, near_source, live, own_charges, first, second,
            near_blocks, raw,
        )

    near = None
    for distance in [2 << i for i in range((per_group // 2).bit_length() - 1)]:
        count = boxes.shape[0]
        got = side_by_side(boxes, groups, functools.partial(swap, axis="dev", distance=distance))
        boxes = jnp.concatenate([boxes, got[:count]])
        groups = groups + got[count:]
        if near is None:
            near, table_high = near_part()
            boxes, groups, near, table_high = lax.optimization_barrier(
                (boxes, groups, near, table_high)
            )

    tables = [
        x.reshape(kinds, x.shape[0] // kinds, 2 * k) for x in (table_low, table_high)
    ]
    wanted = groups.shape[0] - 1 + dev_couple.shape[1]
    far, box_tables, leaf_maps = pl.pallas_call(
        functools.partial(far_kernel, len(tables), tuple(offsets)),
        out_shape=(
            shape((leaves // 2, r, 2 * k), F32),
            shape((wanted * half, 2 * k), F32),
            shape((2, k, trans_leaf.shape[0] * k), BF16),
        ),
        in_specs=[SMEM] * 4 + [VMEM] * (2 + len(tables)),
        out_specs=(VMEM, VMEM, VMEM),
        compiler_params=params(16),
        cost_estimate=cost(3),
        name="far",
    )(
        leaf_far.T, leaf_far_couple.T, dev_couple, grp_couple, spread, leaf_maps, *tables
    )

    return pl.pallas_call(
        functools.partial(final_kernel, 8),
        out_shape=shape((leaves, r, panels), F32),
        in_specs=[SMEM] * 3 + [VMEM] * 8,
        out_specs=HBM,
        scratch_shapes=[
            pltpu.VMEM((leaves, r, panels), F32),
            pltpu.VMEM((trans_leaf.shape[0], r, 2 * k), F32),
            pltpu.SemaphoreType.DMA((8,)),
        ],
        compiler_params=params(16),
        name="final",
    )(
        leaf_kinds, dev_kind, dev_list, near, far, box_tables, boxes, groups, basis,
        leaf_maps, dev_maps,
    )


def solution(mesh):
    leaf = P(AXES)
    return jax.shard_map(
        local,
        mesh=mesh,
        in_specs=(leaf,) * 12 + (P(),) * 4,
        out_specs=leaf,
        check_vma=False,
    )
```

```python
import functools

import jax
import jax.numpy as jnp
from jax import lax
from jax.experimental import pallas as pl
from jax.experimental.pallas import tpu as pltpu
from jax.sharding import PartitionSpec as P

F32 = jnp.float32
BF16 = jnp.bfloat16
NT = (((1,), (1,)), ((), ()))
AXES = ("grp", "dev")
VMEM = pl.BlockSpec(memory_space=pltpu.VMEM)
SMEM = pl.BlockSpec(memory_space=pltpu.SMEM)
HBM = pl.BlockSpec(memory_space=pltpu.HBM)
MIB = 2**20
TABLE_ROWS = 8
PIECES = 4


def halves(x):
    half = x.shape[1] // 2
    return jnp.concatenate([x[:, :half], x[:, half:]], axis=0)


def fold(product):
    r, j = product.shape[0] // 2, product.shape[1] // 2
    return product[:r, :j] + product[r:, j:]


def split(x):
    high = x.astype(BF16)
    return high, (x - high.astype(F32)).astype(BF16)


def dot3(a, b, dims=(((1,), (0,)), ((), ()))):
    (a_high, a_low), (b_high, b_low) = split(a), split(b)
    both = lax.dot_general(
        jnp.concatenate([a_high, a_low], axis=0), b_high, dims, preferred_element_type=F32
    )
    rest = lax.dot_general(a_high, b_low, dims, preferred_element_type=F32)
    return both[: a.shape[0]] + both[a.shape[0] :] + rest


def moment_kernel(
    leaf_trans_hbm, dev_trans, charges_hbm, basis_hbm, trans_leaf_hbm, trans_dev_hbm, table_hbm,
    moments, send_first, send_second, sums, leaf_trans, dev_trans_out, charges, basis_t,
    trans_leaf, trans_dev, table, classes, sems,
):
    leaves, r, _ = charges.shape
    k = basis_t.shape[1]
    margin = leaves // 2
    kinds = trans_leaf.shape[0]
    size = leaves // PIECES
    moves = [(basis_hbm, basis_t), (charges_hbm, charges), (leaf_trans_hbm, leaf_trans)]
    moves += [(trans_leaf_hbm, trans_leaf), (trans_dev_hbm, trans_dev)]
    moves += [
        (table_hbm.at[:, pl.ds(i, TABLE_ROWS)], table.at[:, pl.ds(i, TABLE_ROWS)])
        for i in range(0, table.shape[1], TABLE_ROWS)
    ]
    copies = [
        pltpu.make_async_copy(source, target, sems.at[i])
        for i, (source, target) in enumerate(moves)
    ]
    for copy in copies:
        copy.start()
    even = lax.rem(lax.axis_index("dev"), 2) == 0
    left = lax.broadcasted_iota(jnp.int32, (r, 2 * k), 1) < k
    for lane in range(PIECES):
        classes[lane][...] = jnp.zeros_like(classes[lane])
    for copy in copies[:3]:
        copy.wait()
    panels = charges.shape[2]
    for start in range(0, leaves, PIECES):
        product = lax.dot_general(
            charges[start : start + PIECES].reshape(PIECES * r, panels),
            basis_t[start : start + PIECES].reshape(PIECES * k, panels), NT,
            preferred_element_type=F32,
        )
        for u in range(PIECES):
            leaf = start + u
            pair = product[u * r : (u + 1) * r, u // 2 * 2 * k : (u // 2 + 1) * 2 * k]
            turned = pltpu.roll(pair, k, 1)
            twice = jnp.where(left, pair, turned) if u % 2 == 0 else jnp.where(left, turned, pair)
            kind = leaf_trans[leaf]
            lane = classes[u]
            lane[kind] = lane[kind] + twice
            high = twice.astype(BF16).astype(F32)
            moments[leaf] = jnp.where(left, high, twice - high).astype(BF16)
    copies[3].wait()
    copies[4].wait()
    classes = sum([lane[...] for lane in classes[1:]], start=classes[0][...])
    lhs = [
        jnp.where(left, classes[kind], classes[kind + 1]) for kind in range(0, kinds, 2)
    ]
    box = dot3(jnp.concatenate(lhs, axis=1), trans_leaf[...].reshape(kinds * k, k))
    dev_trans_out[0] = dev_trans[0]
    up = dot3(box, trans_dev[dev_trans[0]])
    both = jnp.concatenate([box, up], axis=1)
    sums[...] = both

    def fill(first_from, second_from):
        for leaf in range(margin):
            send_first[leaf, :r] = charges[first_from + leaf]
            send_first[leaf, r:] = moments[first_from + leaf]
            send_second[leaf, :r] = charges[second_from + leaf]
            send_second[leaf, r:] = moments[second_from + leaf]

    @pl.when(even)
    def _():
        fill(margin, 0)

    @pl.when(jnp.logical_not(even))
    def _():
        fill(0, margin)

    for copy in copies[5:]:
        copy.wait()


def relayout(table, row, out, place, count):
    kinds = table.shape[3]
    stacked = jnp.concatenate([table[0, row], table[1, row]], axis=0)
    for start in range(0, kinds, 128):
        width = min(128, kinds - start)
        out[pl.ds(start * count + place, width, stride=count), :] = stacked[
            :, start : start + width
        ].T


def relayout_rows(table, out, begin, count, rows):
    def step(row, carry):
        relayout(table, row, out, begin + row, rows)
        return carry

    lax.fori_loop(0, count, step, 0, unroll=8)


def table_kernel(table, high_hbm, out, high, sems):
    low_rows, high_rows = table.shape[1], high.shape[1]
    copies = [
        pltpu.make_async_copy(
            high_hbm.at[:, pl.ds(low_rows + i, TABLE_ROWS)],
            high.at[:, pl.ds(i, TABLE_ROWS)],
            sems.at[i // TABLE_ROWS],
        )
        for i in range(0, high_rows, TABLE_ROWS)
    ]
    for copy in copies:
        copy.start()
    rows = out.shape[0] // table.shape[3]
    relayout_rows(table, out, 0, low_rows, rows)
    for i, copy in enumerate(copies):
        copy.wait()
        begin = i * TABLE_ROWS
        if low_rows + begin < rows:
            relayout_rows(high.at[:, begin : begin + TABLE_ROWS], out, low_rows + begin, TABLE_ROWS, rows)


def halo_places(leaves):
    margin = leaves // 2
    even = lax.rem(lax.axis_index("dev"), 2) == 0
    return jnp.where(even, margin + leaves, 0), jnp.where(even, 0, margin + leaves)


def first_leaf(leaves):
    return (lax.axis_index("grp") * lax.axis_size("dev") + lax.axis_index("dev")) * leaves


def near_kernel(
    steps, begin, rows, targets, sources, count, charges, first, second, blocks, table, out, table_out,
    window, total,
):
    chunk = blocks.shape[0] // steps
    leaves, r, panels = charges.shape
    margin = leaves // 2
    live = count[...]
    leaf_start = first_leaf(leaves)
    first_at, second_at = halo_places(leaves)
    window[pl.ds(margin, leaves)] = charges[...]
    window[pl.ds(first_at, margin)] = first[:margin, :r]
    window[pl.ds(second_at, margin)] = second[:, :r]
    total[...] = jnp.zeros_like(total)

    def picked(slot):
        return window[sources[slot] - leaf_start + margin]

    def step(index, carry):
        base = index * chunk
        products = []
        empty = jnp.zeros((r, panels), BF16)
        for u in [base + i for i in range(0, chunk, 4)]:
            one, two, three, four = (picked(u + i) for i in range(4))
            lhs = jnp.concatenate([one, empty, three, empty], axis=0)
            rhs = jnp.concatenate([empty, two, empty, four], axis=0)
            both = lax.dot_general(
                jnp.concatenate([lhs, rhs], axis=1),
                jnp.concatenate(
                    [
                        jnp.concatenate([blocks[u], blocks[u + 2]], axis=0),
                        jnp.concatenate([blocks[u + 1], blocks[u + 3]], axis=0),
                    ],
                    axis=1,
                ),
                NT, preferred_element_type=F32,
            )
            products += [both[:r, :panels], both[r : 2 * r, :panels]]
            products += [both[2 * r : 3 * r, panels:], both[3 * r :, panels:]]
        for u in range(rows // steps):
            place = index * (rows // steps) + u
            relayout(table, begin + place, table_out, place, rows)
        for u in range(chunk):
            slot = base + u
            row = targets[slot] - leaf_start
            total[row] = total[row] + jnp.where(live > slot, products[u], 0.0)
        return carry

    lax.fori_loop(0, steps, step, 0)
    out[...] = total[...]


def couple(tables, kind):
    return jnp.concatenate([table[kind] for table in tables], axis=0)


def spread_kernel(count, moments, first, second, spread, count_out, window):
    count_out[...] = jnp.full(count_out.shape, count[0], jnp.int32)
    leaves, r, width = moments.shape
    margin = leaves // 2
    half = width // 4
    first_at, second_at = halo_places(leaves)
    window[pl.ds(margin, leaves)] = moments[...]
    window[pl.ds(first_at, margin)] = first[:margin, r:]
    window[pl.ds(second_at, margin)] = second[:, r:]
    row = lax.broadcasted_iota(jnp.int32, (width, 4 * width), 0)
    column = lax.broadcasted_iota(jnp.int32, (width, 4 * width), 1)
    copier = (row == (column // width) * half + lax.rem(column, half)).astype(BF16)
    piece = 8
    for start in range(0, 2 * leaves, piece):
        rows = window[start : start + piece].reshape(piece * r, width)
        copied = jnp.dot(rows, copier, preferred_element_type=F32).astype(BF16)
        for section in range(4):
            spread[start : start + piece, section * r : (section + 1) * r] = copied[
                :, section * width : (section + 1) * width
            ].reshape(piece, r, width)


def far_kernel(
    parts, offsets, far, far_couple, dev_couple, grp_couple, spread, trans_leaf, *rest
):
    tables = rest[:parts]
    out, box_tables, leaf_maps = rest[parts:]
    pairs, r, width = out.shape
    leaves, k, half = 2 * pairs, width // 2, width // 4
    nfar = far.shape[0]
    group = lax.axis_index("grp")
    origin = first_leaf(leaves) - leaves // 2
    lane = lax.broadcasted_iota(jnp.int32, (4 * r, width), 1) // half
    for leaf in range(leaves):
        lhs, rhs = [], []
        for quad in range(nfar // 4):
            picked = None
            taken = []
            for q in range(4):
                f = quad * 4 + q
                source = spread[far[f, leaf] - origin]
                picked = source if q == 0 else jnp.where(lane >= q, source, picked)
                taken.append(couple(tables, far_couple[f, leaf]))
            lhs.append(picked)
            rhs.append(jnp.concatenate(split(jnp.concatenate(taken, axis=0)), axis=1))
        product = jnp.dot(
            jnp.concatenate(lhs, axis=1), jnp.concatenate(rhs, axis=0),
            preferred_element_type=F32,
        )
        product = product[: 2 * r] + product[2 * r :]
        product = product[:, :width] + product[:, width:]
        own, other = (product[:r], product[r:]) if leaf % 2 == 0 else (product[r:], product[:r])
        folded = own + pltpu.roll(other, k, 1)
        if leaf % 2 == 0:
            even_leaf = folded
        else:
            out[leaf // 2] = jnp.where(lane[:r] < 2, even_leaf, folded)
    for kind in range(0, trans_leaf.shape[0], 2):
        two = trans_leaf[kind : kind + 2].reshape(width, k).T
        high, low = split(two)
        leaf_maps[0, :, kind * k : (kind + 2) * k] = high
        leaf_maps[1, :, kind * k : (kind + 2) * k] = low
    wanted = [
        grp_couple[group, jnp.bitwise_xor(group, other)] for other in offsets[1:]
    ] + [dev_couple[0, n] for n in range(dev_couple.shape[1])]
    for i, kind in enumerate(wanted):
        box_tables[i * half : (i + 1) * half] = couple(tables, kind)


def final_kernel(
    steps, leaf_trans, dev_trans, dev_list, near, far, box_tables, boxes, groups, basis_t,
    leaf_maps, trans_dev, out_hbm, out, locals_, sems,
):
    leaves, r, panels = near.shape
    k = leaf_maps.shape[1]
    kinds = leaf_maps.shape[2] // k
    others = groups.shape[0] - 1
    group = lax.axis_index("grp")
    member = lax.axis_index("dev")
    split_at = others * (k // 2)
    lhs = [halves(groups[other + 1]) for other in range(others)]
    group_local = fold(dot3(jnp.concatenate(lhs, axis=1), box_tables[:split_at]))
    lhs = []
    for n in range(dev_list.shape[1]):
        place = jnp.bitwise_xor(dev_list[0, n] - group * lax.axis_size("dev"), member)
        lhs.append(halves(boxes[place]))
    listed = fold(dot3(jnp.concatenate(lhs, axis=1), box_tables[split_at:]))
    box_local = dot3(group_local, trans_dev[dev_trans[0]], NT) + listed
    high, low = split(box_local)
    by_kind = jnp.dot(
        jnp.concatenate([high, low], axis=0), leaf_maps[0], preferred_element_type=F32
    )
    by_kind = by_kind[:r] + by_kind[r:]
    by_kind += jnp.dot(high, leaf_maps[1], preferred_element_type=F32)
    left = lax.broadcasted_iota(jnp.int32, (r, 2 * k), 1) < k
    for kind in range(0, kinds, 2):
        two = by_kind[:, kind * k : (kind + 2) * k]
        turned = pltpu.roll(two, k, 1)
        locals_[kind] = jnp.where(left, two, turned)
        locals_[kind + 1] = jnp.where(left, turned, two)
    size = leaves // steps
    copies = []
    for i in range(steps):
        for leaf in range(i * size, (i + 1) * size, 4):
            lhs = []
            for u in range(4):
                whole = locals_[leaf_trans[leaf + u]] + far[(leaf + u) // 2]
                lhs.append(jnp.where(left if u % 2 == 0 else jnp.logical_not(left), whole, 0.0))
            rhs = [
                basis_t[leaf + u : leaf + u + 2].reshape(2 * k, panels) for u in range(0, 4, 2)
            ]
            product = jnp.dot(
                jnp.concatenate(lhs, axis=0).astype(BF16), jnp.concatenate(rhs, axis=1),
                preferred_element_type=F32,
            )
            for u in range(4):
                columns = slice(u // 2 * panels, (u // 2 + 1) * panels)
                out[leaf + u] = near[leaf + u] + product[u * r : (u + 1) * r, columns]
        piece = pl.ds(i * size, size)
        copies.append(pltpu.make_async_copy(out.at[piece], out_hbm.at[piece], sems.at[i]))
        copies[-1].start()
    for copy in copies:
        copy.wait()


def swap(x, axis, distance):
    return lax.ppermute(x, axis, [(i, i ^ distance) for i in range(lax.axis_size(axis))])


def side_by_side(first, second, move):
    parts = jnp.concatenate([first, second])
    total, _, k = parts.shape
    half = (total + 1) // 2
    parts = jnp.pad(parts, ((0, 2 * half - total), (0, 0), (0, 0)))
    got = move(jnp.concatenate([parts[:half], parts[half:]], axis=2))
    return jnp.concatenate([got[:, :, :k], got[:, :, k:]])[:total]


def cost(us):
    return pl.CostEstimate(flops=0, bytes_accessed=us * 3 * MIB, transcendentals=0)


def params(mib):
    return pltpu.CompilerParams(vmem_limit_bytes=mib * MIB)


def local(
    charges,
    leaf_basis,
    near_blocks,
    near_target,
    near_source,
    near_count,
    leaf_far,
    leaf_far_couple,
    leaf_trans,
    dev_trans,
    dev_list,
    dev_couple,
    grp_couple,
    trans_leaf,
    trans_dev,
    couple_table,
):
    leaves, r, panels = charges.shape
    k = leaf_basis.shape[2]
    margin = leaves // 2
    slots = near_blocks.shape[0]
    kinds = couple_table.shape[0]
    half = k // 2
    per_group = lax.axis_size("dev")
    devices = per_group * lax.axis_size("grp")
    basis_t = jnp.swapaxes(leaf_basis, 1, 2)
    shape = jax.ShapeDtypeStruct

    couplings = pltpu.with_memory_space_constraint(
        jnp.transpose(couple_table, (1, 2, 0)).reshape(2, half, k, kinds), pltpu.HBM
    )
    (
        moments, send_first, send_second, sums, leaf_kinds, dev_kind, own_charges, basis,
        leaf_maps, dev_maps, raw,
    ) = (
        pl.pallas_call(
            moment_kernel,
            out_shape=(
                shape((leaves, r, 2 * k), BF16),
                shape((margin, 2 * r, panels), BF16),
                shape((margin, 2 * r, panels), BF16),
                shape((r, 2 * k), F32),
                shape(leaf_trans.shape, jnp.int32),
                shape((8,), jnp.int32),
                shape(charges.shape, BF16),
                shape(basis_t.shape, BF16),
                shape(trans_leaf.shape, F32),
                shape(trans_dev.shape, F32),
                shape((2, half // 4, k, kinds), F32),
            ),
            in_specs=[HBM, SMEM] + [HBM] * 5,
            out_specs=(VMEM,) * 4 + (SMEM,) * 2 + (VMEM,) * 5,
            scratch_shapes=[
                [pltpu.VMEM((trans_leaf.shape[0], r, 2 * k), F32) for _ in range(PIECES)],
                pltpu.SemaphoreType.DMA((5 + half // 4 // TABLE_ROWS,)),
            ],
            compiler_params=params(24),
            name="moments",
        )(
            pltpu.with_memory_space_constraint(leaf_trans, pltpu.HBM),
            dev_trans,
            pltpu.with_memory_space_constraint(charges, pltpu.HBM),
            pltpu.with_memory_space_constraint(basis_t, pltpu.HBM),
            pltpu.with_memory_space_constraint(trans_leaf, pltpu.HBM),
            pltpu.with_memory_space_constraint(trans_dev, pltpu.HBM),
            couplings,
        )
    )

    first = swap(send_first, "dev", 1)
    peer = swap(sums, "dev", 1)
    partners = [(i, i + 1) for i in range(1, devices - 1, 2)] + [(0, devices - 1)]
    second = lax.ppermute(send_second, AXES, partners + [(j, i) for i, j in partners])
    boxes = jnp.stack([sums[:, :k], peer[:, :k]])
    groups = (sums + peer)[None, :, k:]
    boxes, groups, raw = lax.optimization_barrier((boxes, groups, raw))
    offsets = [0]
    for distance in [2 << i for i in range((lax.axis_size("grp") // 2).bit_length() - 1)]:
        groups = jnp.concatenate([groups, swap(groups, "grp", distance)])
        offsets += [offset ^ distance for offset in offsets]
    high_rows = half // 4
    low_rows = half - high_rows
    table_low, raw = pl.pallas_call(
        table_kernel,
        out_shape=(
            shape((kinds * low_rows, 2 * k), F32),
            shape((2, half - half // 4, k, kinds), F32),
        ),
        in_specs=[VMEM, HBM],
        out_specs=(VMEM, VMEM),
        scratch_shapes=[pltpu.SemaphoreType.DMA(((half - half // 4) // TABLE_ROWS,))],
        compiler_params=params(16),
        cost_estimate=cost(3),
        name="table",
    )(raw, couplings)
    groups, table_low, first, second = lax.optimization_barrier(
        (groups, table_low, first, second)
    )
    groups = jnp.concatenate([groups, swap(groups, "grp", 1)])
    offsets += [offset ^ 1 for offset in offsets]
    spread, live = pl.pallas_call(
        spread_kernel,
        out_shape=(shape((2 * leaves, 4 * r, 2 * k), BF16), shape((r, panels), jnp.int32)),
        in_specs=[SMEM] + [VMEM] * 3,
        out_specs=(VMEM, VMEM),
        scratch_shapes=[pltpu.VMEM((2 * leaves, r, 2 * k), BF16)],
        compiler_params=params(16),
        cost_estimate=cost(1),
        name="spread",
    )(near_count, moments, first, second)
    groups, spread, live, first, second = lax.optimization_barrier(
        (groups, spread, live, first, second)
    )
    steps = 2

    def near_part():
        return pl.pallas_call(
            functools.partial(near_kernel, steps, low_rows - half // 4, high_rows),
            out_shape=(
                shape((leaves, r, panels), F32),
                shape((kinds * high_rows, 2 * k), F32),
            ),
            in_specs=[SMEM] * 2 + [VMEM] * 6,
            out_specs=(VMEM, VMEM),
            scratch_shapes=[
                pltpu.VMEM((2 * leaves, r, panels), BF16),
                pltpu.VMEM((leaves, r, panels), F32),
            ],
            compiler_params=params(16),
            cost_estimate=cost(3),
            name="near",
        )(
            near_target, near_source, live, own_charges, first, second,
            near_blocks, raw,
        )

    near = None
    for distance in [2 << i for i in range((per_group // 2).bit_length() - 1)]:
        count = boxes.shape[0]
        got = side_by_side(boxes, groups, functools.partial(swap, axis="dev", distance=distance))
        boxes = jnp.concatenate([boxes, got[:count]])
        groups = groups + got[count:]
        if near is None:
            near, table_high = near_part()
            boxes, groups, near, table_high = lax.optimization_barrier(
                (boxes, groups, near, table_high)
            )

    tables = [
        x.reshape(kinds, x.shape[0] // kinds, 2 * k) for x in (table_low, table_high)
    ]
    wanted = groups.shape[0] - 1 + dev_couple.shape[1]
    far, box_tables, leaf_maps = pl.pallas_call(
        functools.partial(far_kernel, len(tables), tuple(offsets)),
        out_shape=(
            shape((leaves // 2, r, 2 * k), F32),
            shape((wanted * half, 2 * k), F32),
            shape((2, k, trans_leaf.shape[0] * k), BF16),
        ),
        in_specs=[SMEM] * 4 + [VMEM] * (2 + len(tables)),
        out_specs=(VMEM, VMEM, VMEM),
        compiler_params=params(16),
        cost_estimate=cost(3),
        name="far",
    )(
        leaf_far.T, leaf_far_couple.T, dev_couple, grp_couple, spread, leaf_maps, *tables
    )

    return pl.pallas_call(
        functools.partial(final_kernel, 8),
        out_shape=shape((leaves, r, panels), F32),
        in_specs=[SMEM] * 3 + [VMEM] * 8,
        out_specs=HBM,
        scratch_shapes=[
            pltpu.VMEM((leaves, r, panels), F32),
            pltpu.VMEM((trans_leaf.shape[0], r, 2 * k), F32),
            pltpu.SemaphoreType.DMA((8,)),
        ],
        compiler_params=params(16),
        name="final",
    )(
        leaf_kinds, dev_kind, dev_list, near, far, box_tables, boxes, groups, basis,
        leaf_maps, dev_maps,
    )


def solution(mesh):
    leaf = P(AXES)
    return jax.shard_map(
        local,
        mesh=mesh,
        in_specs=(leaf,) * 12 + (P(),) * 4,
        out_specs=leaf,
        check_vma=False,
    )
```

```python
import functools

import jax
import jax.numpy as jnp
from jax import lax
from jax.experimental import pallas as pl
from jax.experimental.pallas import tpu as pltpu
from jax.sharding import PartitionSpec as P

F32 = jnp.float32
BF16 = jnp.bfloat16
NT = (((1,), (1,)), ((), ()))
AXES = ("grp", "dev")
VMEM = pl.BlockSpec(memory_space=pltpu.VMEM)
SMEM = pl.BlockSpec(memory_space=pltpu.SMEM)
HBM = pl.BlockSpec(memory_space=pltpu.HBM)
MIB = 2**20
TABLE_ROWS = 4
PIECES = 4


def halves(x):
    half = x.shape[1] // 2
    return jnp.concatenate([x[:, :half], x[:, half:]], axis=0)


def fold(product):
    r, j = product.shape[0] // 2, product.shape[1] // 2
    return product[:r, :j] + product[r:, j:]


def split(x):
    high = x.astype(BF16)
    return high, (x - high.astype(F32)).astype(BF16)


def dot3(a, b, dims=(((1,), (0,)), ((), ()))):
    (a_high, a_low), (b_high, b_low) = split(a), split(b)
    both = lax.dot_general(
        jnp.concatenate([a_high, a_low], axis=0), b_high, dims, preferred_element_type=F32
    )
    rest = lax.dot_general(a_high, b_low, dims, preferred_element_type=F32)
    return both[: a.shape[0]] + both[a.shape[0] :] + rest


def moment_kernel(
    leaf_trans_hbm, dev_trans, charges_hbm, basis_hbm, trans_leaf_hbm, trans_dev_hbm, table_hbm,
    moments, send_first, send_second, sums, leaf_trans, dev_trans_out, charges, basis_t,
    trans_leaf, trans_dev, table, classes, sems,
):
    leaves, r, _ = charges.shape
    k = basis_t.shape[1]
    margin = leaves // 2
    kinds = trans_leaf.shape[0]
    size = leaves // PIECES
    moves = [(basis_hbm, basis_t), (charges_hbm, charges), (leaf_trans_hbm, leaf_trans)]
    moves += [(trans_leaf_hbm, trans_leaf), (trans_dev_hbm, trans_dev)]
    moves += [
        (table_hbm.at[:, pl.ds(i, TABLE_ROWS)], table.at[:, pl.ds(i, TABLE_ROWS)])
        for i in range(0, table.shape[1], TABLE_ROWS)
    ]
    copies = [
        pltpu.make_async_copy(source, target, sems.at[i])
        for i, (source, target) in enumerate(moves)
    ]
    for copy in copies:
        copy.start()
    even = lax.rem(lax.axis_index("dev"), 2) == 0
    left = lax.broadcasted_iota(jnp.int32, (r, 2 * k), 1) < k
    for lane in range(PIECES):
        classes[lane][...] = jnp.zeros_like(classes[lane])
    for copy in copies[:3]:
        copy.wait()
    panels = charges.shape[2]
    for start in range(0, leaves, PIECES):
        product = lax.dot_general(
            charges[start : start + PIECES].reshape(PIECES * r, panels),
            basis_t[start : start + PIECES].reshape(PIECES * k, panels), NT,
            preferred_element_type=F32,
        )
        for u in range(PIECES):
            leaf = start + u
            pair = product[u * r : (u + 1) * r, u // 2 * 2 * k : (u // 2 + 1) * 2 * k]
            turned = pltpu.roll(pair, k, 1)
            twice = jnp.where(left, pair, turned) if u % 2 == 0 else jnp.where(left, turned, pair)
            kind = leaf_trans[leaf]
            lane = classes[u]
            lane[kind] = lane[kind] + twice
            high = twice.astype(BF16).astype(F32)
            moments[leaf] = jnp.where(left, high, twice - high).astype(BF16)
    copies[3].wait()
    copies[4].wait()
    classes = sum([lane[...] for lane in classes[1:]], start=classes[0][...])
    lhs = [
        jnp.where(left, classes[kind], classes[kind + 1]) for kind in range(0, kinds, 2)
    ]
    box = dot3(jnp.concatenate(lhs, axis=1), trans_leaf[...].reshape(kinds * k, k))
    dev_trans_out[0] = dev_trans[0]
    up = dot3(box, trans_dev[dev_trans[0]])
    both = jnp.concatenate([box, up], axis=1)
    sums[...] = both

    def fill(first_from, second_from):
        for leaf in range(margin):
            send_first[leaf, :r] = charges[first_from + leaf]
            send_first[leaf, r:] = moments[first_from + leaf]
            send_second[leaf, :r] = charges[second_from + leaf]
            send_second[leaf, r:] = moments[second_from + leaf]

    @pl.when(even)
    def _():
        fill(margin, 0)

    @pl.when(jnp.logical_not(even))
    def _():
        fill(0, margin)

    for copy in copies[5:]:
        copy.wait()


def relayout(table, row, out, place, count):
    kinds = table.shape[3]
    stacked = jnp.concatenate([table[0, row], table[1, row]], axis=0)
    for start in range(0, kinds, 128):
        width = min(128, kinds - start)
        out[pl.ds(start * count + place, width, stride=count), :] = stacked[
            :, start : start + width
        ].T


def relayout_rows(table, out, begin, count, rows):
    def step(row, carry):
        relayout(table, row, out, begin + row, rows)
        return carry

    lax.fori_loop(0, count, step, 0, unroll=8)


def table_kernel(table, high_hbm, out, high, sems):
    low_rows, high_rows = table.shape[1], high.shape[1]
    copies = [
        pltpu.make_async_copy(
            high_hbm.at[:, pl.ds(low_rows + i, TABLE_ROWS)],
            high.at[:, pl.ds(i, TABLE_ROWS)],
            sems.at[i // TABLE_ROWS],
        )
        for i in range(0, high_rows, TABLE_ROWS)
    ]
    for copy in copies:
        copy.start()
    rows = out.shape[0] // table.shape[3]
    relayout_rows(table, out, 0, low_rows, rows)
    for i, copy in enumerate(copies):
        copy.wait()
        begin = i * TABLE_ROWS
        if low_rows + begin < rows:
            relayout_rows(high.at[:, begin : begin + TABLE_ROWS], out, low_rows + begin, TABLE_ROWS, rows)


def halo_places(leaves):
    margin = leaves // 2
    even = lax.rem(lax.axis_index("dev"), 2) == 0
    return jnp.where(even, margin + leaves, 0), jnp.where(even, 0, margin + leaves)


def first_leaf(leaves):
    return (lax.axis_index("grp") * lax.axis_size("dev") + lax.axis_index("dev")) * leaves


def near_kernel(
    steps, begin, rows, targets, sources, count, charges, first, second, blocks, table, out, table_out,
    window, total,
):
    chunk = blocks.shape[0] // steps
    leaves, r, panels = charges.shape
    margin = leaves // 2
    live = count[...]
    leaf_start = first_leaf(leaves)
    first_at, second_at = halo_places(leaves)
    window[pl.ds(margin, leaves)] = charges[...]
    window[pl.ds(first_at, margin)] = first[:margin, :r]
    window[pl.ds(second_at, margin)] = second[:, :r]
    total[...] = jnp.zeros_like(total)

    def picked(slot):
        return window[sources[slot] - leaf_start + margin]

    def step(index, carry):
        base = index * chunk
        products = []
        empty = jnp.zeros((r, panels), BF16)
        for u in [base + i for i in range(0, chunk, 4)]:
            one, two, three, four = (picked(u + i) for i in range(4))
            lhs = jnp.concatenate([one, empty, three, empty], axis=0)
            rhs = jnp.concatenate([empty, two, empty, four], axis=0)
            both = lax.dot_general(
                jnp.concatenate([lhs, rhs], axis=1),
                jnp.concatenate(
                    [
                        jnp.concatenate([blocks[u], blocks[u + 2]], axis=0),
                        jnp.concatenate([blocks[u + 1], blocks[u + 3]], axis=0),
                    ],
                    axis=1,
                ),
                NT, preferred_element_type=F32,
            )
            products += [both[:r, :panels], both[r : 2 * r, :panels]]
            products += [both[2 * r : 3 * r, panels:], both[3 * r :, panels:]]
        for u in range(rows // steps):
            place = index * (rows // steps) + u
            relayout(table, begin + place, table_out, place, rows)
        for u in range(chunk):
            slot = base + u
            row = targets[slot] - leaf_start
            total[row] = total[row] + jnp.where(live > slot, products[u], 0.0)
        return carry

    lax.fori_loop(0, steps, step, 0)
    out[...] = total[...]


def couple(tables, kind):
    return jnp.concatenate([table[kind] for table in tables], axis=0)


def spread_kernel(count, moments, first, second, spread, count_out, window):
    count_out[...] = jnp.full(count_out.shape, count[0], jnp.int32)
    leaves, r, width = moments.shape
    margin = leaves // 2
    half = width // 4
    first_at, second_at = halo_places(leaves)
    window[pl.ds(margin, leaves)] = moments[...]
    window[pl.ds(first_at, margin)] = first[:margin, r:]
    window[pl.ds(second_at, margin)] = second[:, r:]
    row = lax.broadcasted_iota(jnp.int32, (width, 4 * width), 0)
    column = lax.broadcasted_iota(jnp.int32, (width, 4 * width), 1)
    copier = (row == (column // width) * half + lax.rem(column, half)).astype(BF16)
    piece = 8
    for start in range(0, 2 * leaves, piece):
        rows = window[start : start + piece].reshape(piece * r, width)
        copied = jnp.dot(rows, copier, preferred_element_type=F32).astype(BF16)
        for section in range(4):
            spread[start : start + piece, section * r : (section + 1) * r] = copied[
                :, section * width : (section + 1) * width
            ].reshape(piece, r, width)


def far_kernel(
    parts, offsets, far, far_couple, dev_couple, grp_couple, spread, trans_leaf, *rest
):
    tables = rest[:parts]
    out, box_tables, leaf_maps = rest[parts:]
    pairs, r, width = out.shape
    leaves, k, half = 2 * pairs, width // 2, width // 4
    nfar = far.shape[0]
    group = lax.axis_index("grp")
    origin = first_leaf(leaves) - leaves // 2
    lane = lax.broadcasted_iota(jnp.int32, (4 * r, width), 1) // half
    for leaf in range(leaves):
        lhs, rhs = [], []
        for quad in range(nfar // 4):
            picked = None
            taken = []
            for q in range(4):
                f = quad * 4 + q
                source = spread[far[f, leaf] - origin]
                picked = source if q == 0 else jnp.where(lane >= q, source, picked)
                taken.append(couple(tables, far_couple[f, leaf]))
            lhs.append(picked)
            rhs.append(jnp.concatenate(split(jnp.concatenate(taken, axis=0)), axis=1))
        product = jnp.dot(
            jnp.concatenate(lhs, axis=1), jnp.concatenate(rhs, axis=0),
            preferred_element_type=F32,
        )
        product = product[: 2 * r] + product[2 * r :]
        product = product[:, :width] + product[:, width:]
        own, other = (product[:r], product[r:]) if leaf % 2 == 0 else (product[r:], product[:r])
        folded = own + pltpu.roll(other, k, 1)
        if leaf % 2 == 0:
            even_leaf = folded
        else:
            out[leaf // 2] = jnp.where(lane[:r] < 2, even_leaf, folded)
    for kind in range(0, trans_leaf.shape[0], 2):
        two = trans_leaf[kind : kind + 2].reshape(width, k).T
        high, low = split(two)
        leaf_maps[0, :, kind * k : (kind + 2) * k] = high
        leaf_maps[1, :, kind * k : (kind + 2) * k] = low
    wanted = [
        grp_couple[group, jnp.bitwise_xor(group, other)] for other in offsets[1:]
    ] + [dev_couple[0, n] for n in range(dev_couple.shape[1])]
    for i, kind in enumerate(wanted):
        box_tables[i * half : (i + 1) * half] = couple(tables, kind)


def final_kernel(
    steps, leaf_trans, dev_trans, dev_list, near, far, box_tables, boxes, groups, basis_t,
    leaf_maps, trans_dev, out_hbm, out, locals_, sems,
):
    leaves, r, panels = near.shape
    k = leaf_maps.shape[1]
    kinds = leaf_maps.shape[2] // k
    others = groups.shape[0] - 1
    group = lax.axis_index("grp")
    member = lax.axis_index("dev")
    split_at = others * (k // 2)
    lhs = [halves(groups[other + 1]) for other in range(others)]
    group_local = fold(dot3(jnp.concatenate(lhs, axis=1), box_tables[:split_at]))
    lhs = []
    for n in range(dev_list.shape[1]):
        place = jnp.bitwise_xor(dev_list[0, n] - group * lax.axis_size("dev"), member)
        lhs.append(halves(boxes[place]))
    listed = fold(dot3(jnp.concatenate(lhs, axis=1), box_tables[split_at:]))
    box_local = dot3(group_local, trans_dev[dev_trans[0]], NT) + listed
    high, low = split(box_local)
    by_kind = jnp.dot(
        jnp.concatenate([high, low], axis=0), leaf_maps[0], preferred_element_type=F32
    )
    by_kind = by_kind[:r] + by_kind[r:]
    by_kind += jnp.dot(high, leaf_maps[1], preferred_element_type=F32)
    left = lax.broadcasted_iota(jnp.int32, (r, 2 * k), 1) < k
    for kind in range(0, kinds, 2):
        two = by_kind[:, kind * k : (kind + 2) * k]
        turned = pltpu.roll(two, k, 1)
        locals_[kind] = jnp.where(left, two, turned)
        locals_[kind + 1] = jnp.where(left, turned, two)
    size = leaves // steps
    copies = []
    for i in range(steps):
        for leaf in range(i * size, (i + 1) * size, 4):
            lhs = []
            for u in range(4):
                whole = locals_[leaf_trans[leaf + u]] + far[(leaf + u) // 2]
                lhs.append(jnp.where(left if u % 2 == 0 else jnp.logical_not(left), whole, 0.0))
            rhs = [
                basis_t[leaf + u : leaf + u + 2].reshape(2 * k, panels) for u in range(0, 4, 2)
            ]
            product = jnp.dot(
                jnp.concatenate(lhs, axis=0).astype(BF16), jnp.concatenate(rhs, axis=1),
                preferred_element_type=F32,
            )
            for u in range(4):
                columns = slice(u // 2 * panels, (u // 2 + 1) * panels)
                out[leaf + u] = near[leaf + u] + product[u * r : (u + 1) * r, columns]
        piece = pl.ds(i * size, size)
        copies.append(pltpu.make_async_copy(out.at[piece], out_hbm.at[piece], sems.at[i]))
        copies[-1].start()
    for copy in copies:
        copy.wait()


def swap(x, axis, distance):
    return lax.ppermute(x, axis, [(i, i ^ distance) for i in range(lax.axis_size(axis))])


def side_by_side(first, second, move):
    parts = jnp.concatenate([first, second])
    total, _, k = parts.shape
    half = (total + 1) // 2
    parts = jnp.pad(parts, ((0, 2 * half - total), (0, 0), (0, 0)))
    got = move(jnp.concatenate([parts[:half], parts[half:]], axis=2))
    return jnp.concatenate([got[:, :, :k], got[:, :, k:]])[:total]


def cost(us):
    return pl.CostEstimate(flops=0, bytes_accessed=us * 3 * MIB, transcendentals=0)


def params(mib):
    return pltpu.CompilerParams(vmem_limit_bytes=mib * MIB)


def local(
    charges,
    leaf_basis,
    near_blocks,
    near_target,
    near_source,
    near_count,
    leaf_far,
    leaf_far_couple,
    leaf_trans,
    dev_trans,
    dev_list,
    dev_couple,
    grp_couple,
    trans_leaf,
    trans_dev,
    couple_table,
):
    leaves, r, panels = charges.shape
    k = leaf_basis.shape[2]
    margin = leaves // 2
    slots = near_blocks.shape[0]
    kinds = couple_table.shape[0]
    half = k // 2
    per_group = lax.axis_size("dev")
    devices = per_group * lax.axis_size("grp")
    basis_t = jnp.swapaxes(leaf_basis, 1, 2)
    shape = jax.ShapeDtypeStruct

    couplings = pltpu.with_memory_space_constraint(
        jnp.transpose(couple_table, (1, 2, 0)).reshape(2, half, k, kinds), pltpu.HBM
    )
    (
        moments, send_first, send_second, sums, leaf_kinds, dev_kind, own_charges, basis,
        leaf_maps, dev_maps, raw,
    ) = (
        pl.pallas_call(
            moment_kernel,
            out_shape=(
                shape((leaves, r, 2 * k), BF16),
                shape((margin, 2 * r, panels), BF16),
                shape((margin, 2 * r, panels), BF16),
                shape((r, 2 * k), F32),
                shape(leaf_trans.shape, jnp.int32),
                shape((8,), jnp.int32),
                shape(charges.shape, BF16),
                shape(basis_t.shape, BF16),
                shape(trans_leaf.shape, F32),
                shape(trans_dev.shape, F32),
                shape((2, half // 8, k, kinds), F32),
            ),
            in_specs=[HBM, SMEM] + [HBM] * 5,
            out_specs=(VMEM,) * 4 + (SMEM,) * 2 + (VMEM,) * 5,
            scratch_shapes=[
                [pltpu.VMEM((trans_leaf.shape[0], r, 2 * k), F32) for _ in range(PIECES)],
                pltpu.SemaphoreType.DMA((5 + half // 8 // TABLE_ROWS,)),
            ],
            compiler_params=params(24),
            name="moments",
        )(
            pltpu.with_memory_space_constraint(leaf_trans, pltpu.HBM),
            dev_trans,
            pltpu.with_memory_space_constraint(charges, pltpu.HBM),
            pltpu.with_memory_space_constraint(basis_t, pltpu.HBM),
            pltpu.with_memory_space_constraint(trans_leaf, pltpu.HBM),
            pltpu.with_memory_space_constraint(trans_dev, pltpu.HBM),
            couplings,
        )
    )

    first = swap(send_first, "dev", 1)
    peer = swap(sums, "dev", 1)
    partners = [(i, i + 1) for i in range(1, devices - 1, 2)] + [(0, devices - 1)]
    second = lax.ppermute(send_second, AXES, partners + [(j, i) for i, j in partners])
    boxes = jnp.stack([sums[:, :k], peer[:, :k]])
    groups = (sums + peer)[None, :, k:]
    boxes, groups, raw = lax.optimization_barrier((boxes, groups, raw))
    offsets = [0]
    for distance in [2 << i for i in range((lax.axis_size("grp") // 2).bit_length() - 1)]:
        groups = jnp.concatenate([groups, swap(groups, "grp", distance)])
        offsets += [offset ^ distance for offset in offsets]
    high_rows = half // 4
    low_rows = half - high_rows
    table_low, raw = pl.pallas_call(
        table_kernel,
        out_shape=(
            shape((kinds * low_rows, 2 * k), F32),
            shape((2, half - half // 8, k, kinds), F32),
        ),
        in_specs=[VMEM, HBM],
        out_specs=(VMEM, VMEM),
        scratch_shapes=[pltpu.SemaphoreType.DMA(((half - half // 8) // TABLE_ROWS,))],
        compiler_params=params(16),
        cost_estimate=cost(3),
        name="table",
    )(raw, couplings)
    groups, table_low, first, second = lax.optimization_barrier(
        (groups, table_low, first, second)
    )
    groups = jnp.concatenate([groups, swap(groups, "grp", 1)])
    offsets += [offset ^ 1 for offset in offsets]
    spread, live = pl.pallas_call(
        spread_kernel,
        out_shape=(shape((2 * leaves, 4 * r, 2 * k), BF16), shape((r, panels), jnp.int32)),
        in_specs=[SMEM] + [VMEM] * 3,
        out_specs=(VMEM, VMEM),
        scratch_shapes=[pltpu.VMEM((2 * leaves, r, 2 * k), BF16)],
        compiler_params=params(16),
        cost_estimate=cost(1),
        name="spread",
    )(near_count, moments, first, second)
    groups, spread, live, first, second = lax.optimization_barrier(
        (groups, spread, live, first, second)
    )
    steps = 2

    def near_part():
        return pl.pallas_call(
            functools.partial(near_kernel, steps, low_rows - half // 8, high_rows),
            out_shape=(
                shape((leaves, r, panels), F32),
                shape((kinds * high_rows, 2 * k), F32),
            ),
            in_specs=[SMEM] * 2 + [VMEM] * 6,
            out_specs=(VMEM, VMEM),
            scratch_shapes=[
                pltpu.VMEM((2 * leaves, r, panels), BF16),
                pltpu.VMEM((leaves, r, panels), F32),
            ],
            compiler_params=params(16),
            cost_estimate=cost(3),
            name="near",
        )(
            near_target, near_source, live, own_charges, first, second,
            near_blocks, raw,
        )

    near = None
    for distance in [2 << i for i in range((per_group // 2).bit_length() - 1)]:
        count = boxes.shape[0]
        got = side_by_side(boxes, groups, functools.partial(swap, axis="dev", distance=distance))
        boxes = jnp.concatenate([boxes, got[:count]])
        groups = groups + got[count:]
        if near is None:
            near, table_high = near_part()
            boxes, groups, near, table_high = lax.optimization_barrier(
                (boxes, groups, near, table_high)
            )

    tables = [
        x.reshape(kinds, x.shape[0] // kinds, 2 * k) for x in (table_low, table_high)
    ]
    wanted = groups.shape[0] - 1 + dev_couple.shape[1]
    far, box_tables, leaf_maps = pl.pallas_call(
        functools.partial(far_kernel, len(tables), tuple(offsets)),
        out_shape=(
            shape((leaves // 2, r, 2 * k), F32),
            shape((wanted * half, 2 * k), F32),
            shape((2, k, trans_leaf.shape[0] * k), BF16),
        ),
        in_specs=[SMEM] * 4 + [VMEM] * (2 + len(tables)),
        out_specs=(VMEM, VMEM, VMEM),
        compiler_params=params(16),
        cost_estimate=cost(3),
        name="far",
    )(
        leaf_far.T, leaf_far_couple.T, dev_couple, grp_couple, spread, leaf_maps, *tables
    )

    return pl.pallas_call(
        functools.partial(final_kernel, 8),
        out_shape=shape((leaves, r, panels), F32),
        in_specs=[SMEM] * 3 + [VMEM] * 8,
        out_specs=HBM,
        scratch_shapes=[
            pltpu.VMEM((leaves, r, panels), F32),
            pltpu.VMEM((trans_leaf.shape[0], r, 2 * k), F32),
            pltpu.SemaphoreType.DMA((8,)),
        ],
        compiler_params=params(16),
        name="final",
    )(
        leaf_kinds, dev_kind, dev_list, near, far, box_tables, boxes, groups, basis,
        leaf_maps, dev_maps,
    )


def solution(mesh):
    leaf = P(AXES)
    return jax.shard_map(
        local,
        mesh=mesh,
        in_specs=(leaf,) * 12 + (P(),) * 4,
        out_specs=leaf,
        check_vma=False,
    )
```
